1024 devices in a mesh: blk: 32 (over y_lo, z), rep: 32 (over x, y_hi, core).
Axes of the slice: x: 8, y: 8 (y_hi: 2, y_lo: 4; y = y_hi * 4 + y_lo), z: 8, core: 2. Of those that a mesh axis runs over, the one named last changes fastest.
Arguments:
- features: bfloat16 [131072, 128], P(('blk', 'rep')), may hold values from -6 to 6
- weight: bfloat16 [128, 256], replicated, may hold values from -0.5 to 0.5
- cotangent: bfloat16 [131072, 256], P(('blk', 'rep')), may hold values from -6 to 6
- tile_vals: bfloat16 [32, 32, 32, 2, 128, 128], P('blk', 'rep'), may hold values from -0.09375 to 0.09375
- tile_row: int32 [32, 32, 32, 2], P('blk', 'rep'), may hold values from 0 to 31
- tile_count: int32 [32, 32, 32], P('blk', 'rep'), may hold values from 0 to 2, as said below
Outputs:
- activations: bfloat16 [131072, 256], P(('blk', 'rep'))
- feature_grad: bfloat16 [131072, 128], P(('blk', 'rep'))
- weight_grad: float32 [128, 256], replicated
The draws below stay inside these ranges and needn't reach their ends.
Inputs may be any that keep to these rules, and one draw needn't show every extreme that they name: tile_count equals 2 wherever the column block j equals the row block b.
All inputs are finite; a program needn't handle non-finite values.
Results may differ from the reference program's by a relative error of at most 0.03.
Values may be sent and summed in bfloat16 or wider, within the bound.
No kernel may reach another device: no remote copies, remote signals or barrier semaphores. Data moves between devices by JAX's collectives and lax.ppermute only.
A program may use at most 32 MiB of HBM per device.

```python
import jax
import jax.numpy as jnp
from jax import lax

F_IN = 128
F_OUT = 256
R_DEV = 128
MAXT = 2
N_NODES = 131072
N_BLK = 32
N_REP = 32


def draw_tile_count(key, part):
    key = jax.random.fold_in(key, 7)
    key_local, key_device, key_live = jax.random.split(key, 3)
    local_draw = jax.random.randint(key_local, (N_BLK, N_REP, N_BLK), 0, MAXT)
    device_draw = jax.random.randint(key_device, (N_BLK, N_REP, 1), 0, MAXT)
    live_draw = jax.random.randint(key_live, (N_BLK, N_REP, N_BLK), 0, 2)
    tile_total = (1 + jnp.minimum(local_draw, device_draw)) * live_draw
    diagonal_block = jnp.arange(N_BLK)[:, None, None] == jnp.arange(N_BLK)[None, None, :]
    return jnp.where(diagonal_block, MAXT, tile_total).astype(jnp.int32)


def plant(values, rng, least, high):
    shape = values.shape
    index_at = [jax.random.randint(jax.random.fold_in(rng, axis), (), 0, shape[axis]) for axis in range(len(shape))]
    values = values.at[tuple(index_at)].set(least)
    longest = shape.index(max(shape))
    index_at[longest] = (index_at[longest] + 1) % shape[longest]
    return values.at[tuple(index_at)].set(high)


def level_of(key, extent, pieces, smallest, top_value):
    factor_of, own = 1.0, jax.random.fold_in(key, 6)
    for position, blocks in pieces:
        steps = jnp.exp(jax.random.uniform(jax.random.fold_in(own, position), (blocks,), jnp.float32, smallest / len(pieces), top_value / len(pieces)))
        factor_of = factor_of * jnp.repeat(steps, extent[position] // blocks).reshape([-1 if axis == position else 1 for axis in range(len(extent))])
    return factor_of


def normal_values(stream_key, dims, deviation, most, shards=(), held_as=jnp.bfloat16):
    values = deviation * jax.random.normal(stream_key, dims, jnp.float32)
    if shards:
        values = values * level_of(stream_key, dims, shards, -0.22, 0.18)
    return jnp.clip(values, -most, most).astype(held_as)


def setup_inputs(seed: int = 0) -> dict:
    arg_keys = jax.random.split(jax.random.key(seed), 7)
    return {
        "features": normal_values(arg_keys[0], (N_NODES, F_IN), 1.0, 6.0, ((0, 1024),)),
        "weight": normal_values(arg_keys[1], (F_IN, F_OUT), F_IN ** -0.5, 0.5),
        "cotangent": normal_values(arg_keys[2], (N_NODES, F_OUT), 1.0, 6.0, ((0, 1024),)),
        "tile_vals": normal_values(arg_keys[3], (N_BLK, N_REP, N_BLK, MAXT, R_DEV, R_DEV), (N_BLK * R_DEV) ** -0.5, 0.09375, ((0, 32), (1, 32))),
        "tile_row": plant(jax.random.randint(arg_keys[4], (N_BLK, N_REP, N_BLK, MAXT), 0, N_REP), jax.random.fold_in(arg_keys[4], 1), 0, N_REP - 1).astype(jnp.int32),
        "tile_count": draw_tile_count(jax.random.fold_in(arg_keys[6], 71), 0),
    }


def selectors(tile_row, tile_count):
    replica_ids = jnp.arange(N_REP, dtype=jnp.int32)
    slot_ids = jnp.arange(MAXT, dtype=jnp.int32)
    live_slot = slot_ids[None, None, None, :] < tile_count[..., None]
    chosen = (tile_row[..., None] == replica_ids) & live_slot[..., None]
    return chosen.astype(jnp.float32)


def reference(features, weight, cotangent, tile_vals, tile_row, tile_count):
    chosen = selectors(tile_row, tile_count)
    feat_blocks = features.astype(jnp.float32).reshape(N_BLK, N_REP, R_DEV, F_IN)
    highest = lax.Precision.HIGHEST

    def forward_block(block_id):
        def per_replica(replica):
            products = jnp.einsum('jtik,jkf->jtif', tile_vals[block_id, replica].astype(jnp.float32), feat_blocks[:, replica], precision=highest)
            partial_sum = jnp.einsum('jtq,jtif->qif', chosen[block_id, replica], products, precision=highest)
            return lax.optimization_barrier(partial_sum.astype(jnp.bfloat16)).astype(jnp.float32)
        parts = lax.map(per_replica, jnp.arange(N_REP, dtype=jnp.int32))
        return jnp.sum(parts, axis=0)

    aggregated = lax.map(forward_block, jnp.arange(N_BLK, dtype=jnp.int32)).astype(jnp.bfloat16).reshape(N_NODES, F_IN)
    pre = jnp.dot(aggregated, weight, preferred_element_type=jnp.float32)
    activations = jax.nn.silu(pre).astype(jnp.bfloat16)
    sigma = jax.nn.sigmoid(pre)
    grad_pre = (cotangent.astype(jnp.float32) * sigma * (1.0 + pre * (1.0 - sigma))).astype(jnp.bfloat16)
    weight_grad = jnp.dot(aggregated.T, grad_pre, preferred_element_type=jnp.float32)
    grad_agg = jnp.dot(grad_pre, weight.T, preferred_element_type=jnp.float32).astype(jnp.bfloat16)
    grad_blocks = grad_agg.astype(jnp.float32).reshape(N_BLK, N_REP, R_DEV, F_IN)

    def backward_block(running, block_id):
        def per_replica(replica):
            selected = jnp.einsum('jtq,qif->jtif', chosen[block_id, replica], grad_blocks[block_id], precision=highest)
            result = jnp.einsum('jtkc,jtkf->jcf', tile_vals[block_id, replica].astype(jnp.float32), selected, precision=highest)
            return lax.optimization_barrier(result.astype(jnp.bfloat16)).astype(jnp.float32)
        terms = lax.map(per_replica, jnp.arange(N_REP, dtype=jnp.int32))
        return running + terms, None

    start_sum = jnp.zeros((N_REP, N_BLK, R_DEV, F_IN), jnp.float32)
    total, unused = lax.scan(backward_block, start_sum, jnp.arange(N_BLK, dtype=jnp.int32))
    feature_grad = jnp.transpose(total, (1, 0, 2, 3)).reshape(N_NODES, F_IN).astype(jnp.bfloat16)
    return activations, feature_grad, weight_grad
```

```python
import functools

import jax
import jax.numpy as jnp
from jax import lax
from jax.experimental import pallas as pl
from jax.experimental.pallas import tpu as pltpu
from jax.sharding import PartitionSpec as P

VMEM = pl.BlockSpec(memory_space=pltpu.VMEM)
SMEM = pl.BlockSpec(memory_space=pltpu.SMEM)
F32 = jnp.float32
BF16 = jnp.bfloat16


def matmul(a, b):
    return jnp.dot(a, b, preferred_element_type=F32)


def forward_tiles(rows_ref, counts_ref, features_ref, tiles_ref, kept_ref, sent_ref, total):
    parity = lax.rem(lax.axis_index("rep"), 2)
    blocks, slots, side, _ = tiles_ref.shape
    total[...] = jnp.zeros_like(total)
    for j in range(blocks):
        product = matmul(tiles_ref[j].reshape(slots * side, side), features_ref[j])
        for slot in range(slots):
            row = rows_ref[j, slot]
            half = lax.rem(row + parity, 2)
            term = product[slot * side : (slot + 1) * side]
            total[half, row // 2] += jnp.where(slot < counts_ref[j], term, 0.0)
    kept_ref[...] = total[0]
    sent_ref[...] = total[1].astype(sent_ref.dtype)


def dense_layer(parts_ref, weight_ref, cotangent_ref, activations_ref, outgoing_ref):
    groups, side, _ = parts_ref.shape
    aggregated = parts_ref[0].astype(F32)
    for g in range(1, groups):
        aggregated += parts_ref[g].astype(F32)
    aggregated = aggregated.astype(BF16)
    weight = weight_ref[...]
    pre = matmul(aggregated, weight)
    sigma = jax.nn.sigmoid(pre)
    activations_ref[...] = (pre * sigma).astype(BF16)
    grad_pre = cotangent_ref[...].astype(F32) * sigma * (1.0 + pre * (1.0 - sigma))
    grad_pre = grad_pre.astype(BF16)
    grad_agg = lax.dot_general(
        weight, grad_pre, (((1,), (1,)), ((), ())), preferred_element_type=F32
    ).astype(BF16)
    term = lax.dot_general(
        aggregated, grad_pre, (((0,), (0,)), ((), ())), preferred_element_type=F32
    )
    lines = term.shape[0] // groups
    for g in range(groups):
        outgoing_ref[g, :side] = grad_agg
        piece = term[g * lines : (g + 1) * lines]
        outgoing_ref[g, side:] = jnp.concatenate([piece[:, :side], piece[:, side:]], axis=0).astype(BF16)


def backward_tiles(rows_ref, counts_ref, own_ref, other_ref, tiles_ref, outgoing_ref):
    parity = lax.rem(lax.axis_index("rep"), 2)
    blocks, slots, side, _ = tiles_ref.shape
    groups = own_ref.shape[0]
    weight_sum = own_ref[0, side:].astype(F32) + other_ref[0, side:].astype(F32)
    for g in range(1, groups):
        weight_sum += own_ref[g, side:].astype(F32) + other_ref[g, side:].astype(F32)
    lines = weight_sum.shape[0] // 2
    mine = jnp.where(parity == 0, weight_sum[:lines], weight_sum[lines:])
    high = mine.astype(BF16).astype(F32)
    carried = jnp.concatenate([high, mine - high], axis=0).astype(BF16)
    for j in range(blocks):
        picked = []
        for slot in range(slots):
            row = rows_ref[j, slot]
            place = row // 2
            use_own = lax.rem(row + parity, 2) == 0
            live = slot < counts_ref[j]
            block = jnp.where(use_own, own_ref[place, :side], other_ref[place, :side])
            picked.append(jnp.where(live, block, jnp.zeros_like(block)))
        term = matmul(jnp.concatenate(picked, axis=1), tiles_ref[j].reshape(slots * side, side))
        outgoing_ref[j, :side] = term.astype(BF16)
        outgoing_ref[j, side:] = carried


def final_sums(parts_ref, feature_grad_ref, weight_ref):
    blocks, extent, side = parts_ref.shape
    total = parts_ref[0].astype(F32)
    for b in range(1, blocks):
        total += parts_ref[b].astype(F32)
    feature_grad_ref[...] = total[:side].T.astype(BF16)
    lines = (extent - side) // 2
    piece = total[side : side + lines] + total[side + lines :]
    for r in range(weight_ref.shape[0]):
        weight_ref[r] = piece


def call(kernel, inputs, outputs, scratch=()):
    return pl.pallas_call(
        kernel,
        out_shape=outputs,
        in_specs=inputs,
        out_specs=[VMEM] * len(outputs),
        scratch_shapes=scratch,
        compiler_params=pltpu.CompilerParams(vmem_limit_bytes=32 * 2**20),
    )


def local(blocks, replicas, features, weight, cotangent, tile_vals, tile_row, tile_count):
    shape = jax.ShapeDtypeStruct
    side, width = features.shape
    slots = tile_vals.shape[3]
    groups = replicas // 2
    lines = 2 * (weight.shape[0] // groups)
    tiles, rows, counts = tile_vals[0, 0], tile_row[0, 0], tile_count[0, 0]
    same_core = [[2 * g + c for g in range(groups)] for c in range(2)]
    swap = [(r, r ^ 1) for r in range(replicas)]

    def exchange(block, axis, index_groups=None):
        return lax.all_to_all(block, axis, 0, 0, axis_index_groups=index_groups, tiled=True)

    with jax.named_scope("gather_features"):
        gathered = exchange(jnp.broadcast_to(features[None], (blocks, side, width)), "blk")
    kept, sent = call(
        forward_tiles,
        [SMEM, SMEM, VMEM, VMEM],
        [shape((groups, side, width), F32), shape((groups, side, width), BF16)],
        [pltpu.VMEM((2, groups, side, width), F32)],
    )(rows, counts, gathered, tiles)
    with jax.named_scope("sum_partials"):
        pair = (kept + lax.ppermute(sent, "rep", swap).astype(F32)).astype(BF16)
        parts = exchange(pair, "rep", same_core)
    activations, outgoing = call(
        dense_layer,
        [VMEM] * 3,
        [shape((side, weight.shape[1]), BF16), shape((groups, side + lines, width), BF16)],
    )(parts, weight, cotangent)
    with jax.named_scope("gather_grads"):
        own = exchange(outgoing, "rep", same_core)
        other = lax.ppermute(own, "rep", swap)
    (terms,) = call(
        backward_tiles,
        [SMEM, SMEM, VMEM, VMEM, VMEM],
        [shape((blocks, side + lines, width), BF16)],
    )(rows, counts, own, other, tiles)
    with jax.named_scope("sum_terms"):
        arrived = exchange(terms, "blk")
    feature_grad, piece = call(
        final_sums,
        [VMEM],
        [shape((side, width), BF16), shape((replicas, lines // 2, width), F32)],
    )(arrived)
    with jax.named_scope("gather_weight_grad"):
        pieces = exchange(piece, "rep").reshape(groups, 2, lines // 2, width)
    weight_grad = pieces.transpose(0, 2, 1, 3).reshape(weight.shape)
    return activations, feature_grad, weight_grad


def solution(mesh):
    in_specs = (
        P(("blk", "rep"), None),
        P(),
        P(("blk", "rep"), None),
        P("blk", "rep", None, None, None, None),
        P("blk", "rep", None, None),
        P("blk", "rep", None),
    )
    out_specs = (P(("blk", "rep"), None), P(("blk", "rep"), None), P())
    step = functools.partial(local, mesh.shape["blk"], mesh.shape["rep"])
    return jax.shard_map(step, mesh=mesh, in_specs=in_specs, out_specs=out_specs, check_vma=False)
```

```python
import functools

import jax
import jax.numpy as jnp
from jax import lax
from jax.experimental import pallas as pl
from jax.experimental.pallas import tpu as pltpu
from jax.sharding import PartitionSpec as P

VMEM = pl.BlockSpec(memory_space=pltpu.VMEM)
SMEM = pl.BlockSpec(memory_space=pltpu.SMEM)
F32 = jnp.float32
BF16 = jnp.bfloat16


def block_of(near, far, blocks):
    y_near, z_near = divmod(near, 2)
    y_far, z_far = divmod(far, blocks // 8)
    return ((y_far * 2 + y_near) * (blocks // 8) + z_far) * 2 + z_near


def matmul(a, b):
    return jnp.dot(a, b, preferred_element_type=F32)


def spread(block_ref, copies_ref):
    for k in range(copies_ref.shape[0]):
        copies_ref[k] = block_ref[...]


def owner_of(row, rep):
    half = lax.rem(row + rep, 2)
    x_near = lax.rem(row // 4, 2)
    place = (row // 8) * 2 + lax.rem(row // 2, 2)
    return half, x_near, place


def forward_tiles(rows_ref, counts_ref, features_ref, tiles_ref, kept_ref, sent_ref, total):
    rep = lax.axis_index("rep")
    blocks, slots, side, _ = tiles_ref.shape
    total[...] = jnp.zeros_like(total)
    for near in range(features_ref.shape[0]):
        for far in range(features_ref.shape[1]):
            j = block_of(near, far, blocks)
            product = matmul(tiles_ref[j].reshape(slots * side, side), features_ref[near, far])
            for slot in range(slots):
                half, x_near, place = owner_of(rows_ref[j, slot], rep)
                term = product[slot * side : (slot + 1) * side]
                total[half, x_near, place] += jnp.where(slot < counts_ref[j], term, 0.0)
    kept_ref[...] = total[0]
    sent_ref[...] = total[1].astype(sent_ref.dtype)


def dense_layer(parts_ref, weight_ref, cotangent_ref, activations_ref, outgoing_ref):
    places, side, _ = parts_ref.shape
    aggregated = parts_ref[0].astype(F32)
    for g in range(1, places):
        aggregated += parts_ref[g].astype(F32)
    aggregated = aggregated.astype(BF16)
    weight = weight_ref[...]
    pre = matmul(aggregated, weight)
    sigma = jax.nn.sigmoid(pre)
    activations_ref[...] = (pre * sigma).astype(BF16)
    grad_pre = cotangent_ref[...].astype(F32) * sigma * (1.0 + pre * (1.0 - sigma))
    grad_pre = grad_pre.astype(BF16)
    grad_agg = lax.dot_general(
        weight, grad_pre, (((1,), (1,)), ((), ())), preferred_element_type=F32
    ).astype(BF16)
    term = lax.dot_general(
        aggregated, grad_pre, (((0,), (0,)), ((), ())), preferred_element_type=F32
    )
    lines = term.shape[0] // places
    for g in range(places):
        outgoing_ref[g, :side] = grad_agg
        piece = term[g * lines : (g + 1) * lines]
        outgoing_ref[g, side:] = jnp.concatenate([piece[:, :side], piece[:, side:]], axis=0).astype(BF16)


def relay_grads(arrived_ref, outgoing_ref):
    places, extent, side = arrived_ref.shape
    weight_sum = arrived_ref[0, side:].astype(F32)
    for g in range(1, places):
        weight_sum += arrived_ref[g, side:].astype(F32)
    lines = (extent - side) // 2
    for k in range(2):
        for g in range(places):
            outgoing_ref[k, g * side : (g + 1) * side] = arrived_ref[g, :side]
        outgoing_ref[k, places * side :] = weight_sum[k * lines : (k + 1) * lines].astype(BF16)


def backward_tiles(rows_ref, counts_ref, own_ref, other_ref, tiles_ref, outgoing_ref):
    rep = lax.axis_index("rep")
    blocks, slots, side, _ = tiles_ref.shape
    nears, extent, _ = outgoing_ref.shape
    fars = blocks // nears
    grads = (own_ref.shape[1] // side) * side
    own_sum = own_ref[0, grads:].astype(F32) + own_ref[1, grads:].astype(F32)
    other_sum = other_ref[0, grads:].astype(F32) + other_ref[1, grads:].astype(F32)
    carried = (own_sum + other_sum).astype(BF16)
    for near in range(nears):
        for far in range(fars):
            j = block_of(near, far, blocks)
            picked = []
            for slot in range(slots):
                half, x_near, place = owner_of(rows_ref[j, slot], rep)
                nodes = pl.ds(pl.multiple_of(place * side, side), side)
                block = jnp.where(half == 0, own_ref[x_near, nodes], other_ref[x_near, nodes])
                picked.append(jnp.where(slot < counts_ref[j], block, jnp.zeros_like(block)))
            term = matmul(jnp.concatenate(picked, axis=1), tiles_ref[j].reshape(slots * side, side))
            outgoing_ref[near, far * side : (far + 1) * side] = term.astype(BF16)
        outgoing_ref[near, fars * side :] = carried


def relay_terms(arrived_ref, outgoing_ref):
    nears, _, side = arrived_ref.shape
    fars = outgoing_ref.shape[0]
    total = arrived_ref[0].astype(F32)
    for k in range(1, nears):
        total += arrived_ref[k].astype(F32)
    total = total.astype(BF16)
    for g in range(fars):
        outgoing_ref[g, :side] = total[g * side : (g + 1) * side]
        outgoing_ref[g, side:] = total[fars * side :]


def final_sums(parts_ref, feature_grad_ref, weight_ref):
    fars, _, side = parts_ref.shape
    total = parts_ref[0].astype(F32)
    for k in range(1, fars):
        total += parts_ref[k].astype(F32)
    feature_grad_ref[...] = total[:side].T.astype(BF16)
    for r in range(weight_ref.shape[0]):
        weight_ref[r] = total[side:]


def call(kernel, inputs, outputs, scratch=()):
    return pl.pallas_call(
        kernel,
        out_shape=outputs,
        in_specs=inputs,
        out_specs=[VMEM] * len(outputs),
        scratch_shapes=scratch,
        compiler_params=pltpu.CompilerParams(vmem_limit_bytes=32 * 2**20),
    )


def local(blocks, replicas, features, weight, cotangent, tile_vals, tile_row, tile_count):
    def shape(*dims, dtype=BF16):
        return jax.ShapeDtypeStruct(dims, dtype)

    side, width = features.shape
    hidden = weight.shape[1]
    nears, fars = 4, blocks // 4
    x_fars, places = replicas // 8, replicas // 4
    lines = weight.shape[0] // places
    tiles, rows, counts = tile_vals[0, 0], tile_row[0, 0], tile_count[0, 0]

    near_blocks = [[block_of(k, g, blocks) for k in range(nears)] for g in range(fars)]
    far_blocks = [[block_of(k, g, blocks) for g in range(fars)] for k in range(nears)]

    def rep_of(x_far, x_near, y_hi, core):
        return ((x_far * 2 + x_near) * 2 + y_hi) * 2 + core

    pairs = [(0, 0), (0, 1), (1, 0), (1, 1)]
    near_x = [[rep_of(f, n, y, c) for n in range(2)] for f in range(x_fars) for y, c in pairs]
    far_x = [[rep_of(f, n, y, c) for f in range(x_fars) for y in range(2)] for n, c in pairs]
    same_core = [[2 * g + c for g in range(replicas // 2)] for c in range(2)]
    swap = [(r, r ^ 1) for r in range(replicas)]

    def exchange(block, axis, index_groups):
        return lax.all_to_all(block, axis, 0, 0, axis_index_groups=index_groups, tiled=True)

    with jax.named_scope("gather_features"):
        (copies,) = call(spread, [VMEM], [shape(fars, side, width)])(features)
        band = exchange(copies, "blk", far_blocks)
        (copies,) = call(spread, [VMEM], [shape(nears, fars, side, width)])(band)
        gathered = exchange(copies, "blk", near_blocks)
    kept, sent = call(
        forward_tiles,
        [SMEM, SMEM, VMEM, VMEM],
        [shape(2, places, side, width, dtype=F32), shape(2, places, side, width)],
        [pltpu.VMEM((2, 2, places, side, width), F32)],
    )(rows, counts, gathered, tiles)
    with jax.named_scope("sum_partials"):
        pair = (kept + lax.ppermute(sent, "rep", swap).astype(F32)).astype(BF16)
        near_sum = jnp.sum(exchange(pair, "rep", near_x).astype(F32), axis=0).astype(BF16)
        parts = exchange(near_sum, "rep", far_x)
    activations, outgoing = call(
        dense_layer,
        [VMEM] * 3,
        [shape(side, hidden), shape(places, side + 2 * lines, width)],
    )(parts, weight, cotangent)
    with jax.named_scope("gather_grads"):
        arrived = exchange(outgoing, "rep", far_x)
        (outgoing,) = call(relay_grads, [VMEM], [shape(2, places * side + lines, width)])(arrived)
        own = exchange(outgoing, "rep", near_x)
        other = lax.ppermute(own, "rep", swap)
    (terms,) = call(
        backward_tiles,
        [SMEM, SMEM, VMEM, VMEM, VMEM],
        [shape(nears, fars * side + lines, width)],
    )(rows, counts, own, other, tiles)
    with jax.named_scope("sum_terms"):
        arrived = exchange(terms, "blk", near_blocks)
        (terms,) = call(relay_terms, [VMEM], [shape(fars, side + lines, width)])(arrived)
        arrived = exchange(terms, "blk", far_blocks)
    feature_grad, piece = call(
        final_sums,
        [VMEM],
        [shape(side, width), shape(2 * places, lines, width, dtype=F32)],
    )(arrived)
    with jax.named_scope("gather_weight_grad"):
        pieces = exchange(piece, "rep", same_core).reshape(x_fars, 2, 2, lines, width)
    weight_grad = pieces.transpose(0, 2, 3, 1, 4).reshape(weight.shape)
    return activations, feature_grad, weight_grad


def solution(mesh):
    in_specs = (
        P(("blk", "rep"), None),
        P(),
        P(("blk", "rep"), None),
        P("blk", "rep", None, None, None, None),
        P("blk", "rep", None, None),
        P("blk", "rep", None),
    )
    out_specs = (P(("blk", "rep"), None), P(("blk", "rep"), None), P())
    step = functools.partial(local, mesh.shape["blk"], mesh.shape["rep"])
    return jax.shard_map(step, mesh=mesh, in_specs=in_specs, out_specs=out_specs, check_vma=False)
```

```python
import functools

import jax
import jax.numpy as jnp
from jax import lax
from jax.experimental import pallas as pl
from jax.experimental.pallas import tpu as pltpu
from jax.sharding import PartitionSpec as P

VMEM = pl.BlockSpec(memory_space=pltpu.VMEM)
SMEM = pl.BlockSpec(memory_space=pltpu.SMEM)
F32 = jnp.float32
BF16 = jnp.bfloat16


def block_of(near, far, blocks):
    y_near, z_near = divmod(near, 2)
    y_far, z_far = divmod(far, blocks // 8)
    return ((y_far * 2 + y_near) * (blocks // 8) + z_far) * 2 + z_near


def matmul(a, b):
    return jnp.dot(a, b, preferred_element_type=F32)


def spread(block_ref, copies_ref):
    for k in range(copies_ref.shape[0]):
        copies_ref[k] = block_ref[...]


def forward_tiles(rows_ref, counts_ref, features_ref, tiles_ref, kept_ref, sent_ref, total):
    rep = lax.axis_index("rep")
    blocks, slots, side, _ = tiles_ref.shape
    total[...] = jnp.zeros_like(total)
    for near in range(features_ref.shape[0]):
        for far in range(features_ref.shape[1]):
            j = block_of(near, far, blocks)
            product = matmul(tiles_ref[j].reshape(slots * side, side), features_ref[near, far])
            for slot in range(slots):
                row = rows_ref[slot, j]
                term = product[slot * side : (slot + 1) * side]
                total[lax.rem(row + rep, 2), row // 2] += jnp.where(slot < counts_ref[j], term, 0.0)
    kept_ref[...] = total[0]
    sent_ref[...] = total[1].astype(sent_ref.dtype)


def dense_layer(parts_ref, weight_ref, cotangent_ref, activations_ref, outgoing_ref):
    groups, side, _ = parts_ref.shape
    aggregated = parts_ref[0].astype(F32)
    for g in range(1, groups):
        aggregated += parts_ref[g].astype(F32)
    aggregated = aggregated.astype(BF16)
    weight = weight_ref[...]
    pre = matmul(aggregated, weight)
    sigma = jax.nn.sigmoid(pre)
    activations_ref[...] = (pre * sigma).astype(BF16)
    grad_pre = cotangent_ref[...].astype(F32) * sigma * (1.0 + pre * (1.0 - sigma))
    grad_pre = grad_pre.astype(BF16)
    grad_agg = lax.dot_general(
        weight, grad_pre, (((1,), (1,)), ((), ())), preferred_element_type=F32
    ).astype(BF16)
    term = lax.dot_general(
        aggregated, grad_pre, (((0,), (0,)), ((), ())), preferred_element_type=F32
    )
    pieces = [
        term[top : top + 8, left : left + side]
        for top in range(0, term.shape[0], 8)
        for left in range(0, term.shape[1], side)
    ]
    count = len(pieces) // (groups // 2)
    for g in range(groups):
        first = (g // 2) * count
        outgoing_ref[g, :side] = grad_agg
        outgoing_ref[g, side:] = jnp.concatenate(pieces[first : first + count], axis=0).astype(BF16)


def backward_tiles(rows_ref, counts_ref, own_ref, other_ref, tiles_ref, outgoing_ref):
    rep = lax.axis_index("rep")
    blocks, slots, side, _ = tiles_ref.shape
    groups = own_ref.shape[0]
    nears = outgoing_ref.shape[0]
    fars = blocks // nears
    own_sum, other_sum = own_ref[0, side:].astype(F32), other_ref[0, side:].astype(F32)
    for g in range(1, groups):
        own_sum += own_ref[g, side:].astype(F32)
        other_sum += other_ref[g, side:].astype(F32)
    carried = (own_sum + other_sum).astype(BF16)
    for near in range(nears):
        for far in range(fars):
            j = block_of(near, far, blocks)
            picked = []
            for slot in range(slots):
                row = rows_ref[slot, j]
                place = row // 2
                use_own = lax.rem(row + rep, 2) == 0
                block = jnp.where(use_own, own_ref[place, :side], other_ref[place, :side])
                picked.append(jnp.where(slot < counts_ref[j], block, jnp.zeros_like(block)))
            term = matmul(jnp.concatenate(picked, axis=1), tiles_ref[j].reshape(slots * side, side))
            outgoing_ref[near, far * side : (far + 1) * side] = term.astype(BF16)
        outgoing_ref[near, fars * side :] = carried


def relay_terms(arrived_ref, outgoing_ref):
    nears, _, side = arrived_ref.shape
    fars = outgoing_ref.shape[0]
    total = arrived_ref[0].astype(F32)
    for k in range(1, nears):
        total += arrived_ref[k].astype(F32)
    total = total.astype(BF16)
    for g in range(fars):
        outgoing_ref[g, :side] = total[g * side : (g + 1) * side]
        outgoing_ref[g, side:] = total[fars * side :]


def final_sums(parts_ref, feature_grad_ref, weight_ref):
    fars, _, side = parts_ref.shape
    total = parts_ref[0].astype(F32)
    for k in range(1, fars):
        total += parts_ref[k].astype(F32)
    feature_grad_ref[...] = total[:side].T.astype(BF16)
    for x in range(weight_ref.shape[0]):
        weight_ref[x] = total[side:]


def call(kernel, inputs, outputs, scratch=()):
    return pl.pallas_call(
        kernel,
        out_shape=outputs,
        in_specs=inputs,
        out_specs=[VMEM] * len(outputs),
        scratch_shapes=scratch,
        compiler_params=pltpu.CompilerParams(vmem_limit_bytes=32 * 2**20),
    )


def local(blocks, replicas, features, weight, cotangent, tile_vals, tile_row, tile_count):
    def shape(*dims, dtype=BF16):
        return jax.ShapeDtypeStruct(dims, dtype)

    side, width = features.shape
    hidden = weight.shape[1]
    nears, fars = 4, blocks // 4
    groups, x_size = replicas // 2, replicas // 4
    lines = weight.size // x_size // side
    tiles, rows, counts = tile_vals[0, 0], tile_row[0, 0].T, tile_count[0, 0]

    near_blocks = [[block_of(k, g, blocks) for k in range(nears)] for g in range(fars)]
    far_blocks = [[block_of(k, g, blocks) for g in range(fars)] for k in range(nears)]
    same_core = [[2 * g + c for g in range(groups)] for c in range(2)]
    along_x = [[4 * x + k for x in range(x_size)] for k in range(4)]
    swap = [(r, r ^ 1) for r in range(replicas)]

    def exchange(block, axis, index_groups):
        return lax.all_to_all(block, axis, 0, 0, axis_index_groups=index_groups, tiled=True)

    with jax.named_scope("gather_features"):
        (copies,) = call(spread, [VMEM], [shape(fars, side, width)])(features)
        band = exchange(copies, "blk", far_blocks)
        (copies,) = call(spread, [VMEM], [shape(nears, fars, side, width)])(band)
        gathered = exchange(copies, "blk", near_blocks)
    kept, sent = call(
        forward_tiles,
        [SMEM, SMEM, VMEM, VMEM],
        [shape(groups, side, width, dtype=F32), shape(groups, side, width)],
        [pltpu.VMEM((2, groups, side, width), F32)],
    )(rows, counts, gathered, tiles)
    with jax.named_scope("sum_partials"):
        pair = (kept + lax.ppermute(sent, "rep", swap).astype(F32)).astype(BF16)
        parts = exchange(pair, "rep", same_core)
    activations, outgoing = call(
        dense_layer,
        [VMEM] * 3,
        [shape(side, hidden), shape(groups, side + lines, width)],
    )(parts, weight, cotangent)
    with jax.named_scope("gather_grads"):
        own = exchange(outgoing, "rep", same_core)
        other = lax.ppermute(own, "rep", swap)
    (terms,) = call(
        backward_tiles,
        [SMEM, SMEM, VMEM, VMEM, VMEM],
        [shape(nears, fars * side + lines, width)],
    )(rows, counts, own, other, tiles)
    with jax.named_scope("sum_terms"):
        arrived = exchange(terms, "blk", near_blocks)
        (terms,) = call(relay_terms, [VMEM], [shape(fars, side + lines, width)])(arrived)
        arrived = exchange(terms, "blk", far_blocks)
    feature_grad, piece = call(
        final_sums,
        [VMEM],
        [shape(side, width), shape(x_size, lines, width, dtype=F32)],
    )(arrived)
    with jax.named_scope("gather_weight_grad"):
        pieces = exchange(piece, "rep", along_x).reshape(-1, hidden // side, 8, side)
    weight_grad = pieces.transpose(0, 2, 1, 3).reshape(weight.shape)
    return activations, feature_grad, weight_grad


def solution(mesh):
    in_specs = (
        P(("blk", "rep"), None),
        P(),
        P(("blk", "rep"), None),
        P("blk", "rep", None, None, None, None),
        P("blk", "rep", None, None),
        P("blk", "rep", None),
    )
    out_specs = (P(("blk", "rep"), None), P(("blk", "rep"), None), P())
    step = functools.partial(local, mesh.shape["blk"], mesh.shape["rep"])
    return jax.shard_map(step, mesh=mesh, in_specs=in_specs, out_specs=out_specs, check_vma=False)
```

```python
import functools

import jax
import jax.numpy as jnp
from jax import lax
from jax.experimental import pallas as pl
from jax.experimental.pallas import tpu as pltpu
from jax.sharding import PartitionSpec as P

VMEM = pl.BlockSpec(memory_space=pltpu.VMEM)
SMEM = pl.BlockSpec(memory_space=pltpu.SMEM)
F32 = jnp.float32
BF16 = jnp.bfloat16


def block_of(near, far, blocks):
    y_near, z_near = divmod(near, 2)
    y_far, z_far = divmod(far, blocks // 8)
    return ((y_far * 2 + y_near) * (blocks // 8) + z_far) * 2 + z_near


def matmul(a, b):
    return jnp.dot(a, b, preferred_element_type=F32)


def spread(block_ref, copies_ref):
    for k in range(copies_ref.shape[0]):
        copies_ref[k] = block_ref[...]


def forward_tiles(rows_ref, counts_ref, features_ref, tiles_ref, kept_ref, sent_ref, total):
    rep = lax.axis_index("rep")
    blocks, slots, side, _ = tiles_ref.shape
    total[...] = jnp.zeros_like(total)
    for near in range(features_ref.shape[0]):
        for far in range(features_ref.shape[1]):
            j = block_of(near, far, blocks)
            product = matmul(tiles_ref[j].reshape(slots * side, side), features_ref[near, far])
            for slot in range(slots):
                row = rows_ref[slot, j]
                half, near_row, far_row = lax.rem(row + rep, 2), lax.rem(row // 2, 4), row // 8
                term = product[slot * side : (slot + 1) * side]
                total[half, near_row, far_row] += jnp.where(slot < counts_ref[j], term, 0.0)
    kept_ref[...] = total[0]
    sent_ref[...] = total[1].astype(sent_ref.dtype)


def dense_layer(parts_ref, weight_ref, cotangent_ref, activations_ref, outgoing_ref):
    groups, side, _ = parts_ref.shape
    aggregated = parts_ref[0].astype(F32)
    for g in range(1, groups):
        aggregated += parts_ref[g].astype(F32)
    aggregated = aggregated.astype(BF16)
    weight = weight_ref[...]
    pre = matmul(aggregated, weight)
    sigma = jax.nn.sigmoid(pre)
    activations_ref[...] = (pre * sigma).astype(BF16)
    grad_pre = cotangent_ref[...].astype(F32) * sigma * (1.0 + pre * (1.0 - sigma))
    grad_pre = grad_pre.astype(BF16)
    grad_agg = lax.dot_general(
        weight, grad_pre, (((1,), (1,)), ((), ())), preferred_element_type=F32
    ).astype(BF16)
    term = lax.dot_general(
        aggregated, grad_pre, (((0,), (0,)), ((), ())), preferred_element_type=F32
    )
    pieces = [
        term[top : top + 8, left : left + side]
        for top in range(0, term.shape[0], 8)
        for left in range(0, term.shape[1], side)
    ]
    count = len(pieces) // groups
    for g in range(groups):
        outgoing_ref[g, :side] = grad_agg
        slice_ = jnp.concatenate(pieces[g * count : (g + 1) * count], axis=0)
        outgoing_ref[g, side:] = slice_.astype(BF16)


def relay_grads(arrived_ref, outgoing_ref):
    fars, extent, side = arrived_ref.shape
    weight_sum = arrived_ref[0, side:].astype(F32)
    for k in range(1, fars):
        weight_sum += arrived_ref[k, side:].astype(F32)
    weight_sum = weight_sum.astype(BF16)
    lines = (extent - side) // 2
    for near in range(outgoing_ref.shape[0]):
        for far in range(fars):
            outgoing_ref[near, far * side : (far + 1) * side] = arrived_ref[far, :side]
        first = (near // 2) * lines
        outgoing_ref[near, fars * side :] = weight_sum[first : first + lines]


def backward_tiles(rows_ref, counts_ref, own_ref, other_ref, tiles_ref, outgoing_ref):
    rep = lax.axis_index("rep")
    blocks, slots, side, _ = tiles_ref.shape
    nears = outgoing_ref.shape[0]
    fars = blocks // nears
    grads = (lax.axis_size("rep") // 8) * side
    own_sum, other_sum = own_ref[0, grads:].astype(F32), other_ref[0, grads:].astype(F32)
    for k in range(1, own_ref.shape[0]):
        own_sum += own_ref[k, grads:].astype(F32)
        other_sum += other_ref[k, grads:].astype(F32)
    carried = (own_sum + other_sum).astype(BF16)
    for near in range(nears):
        for far in range(fars):
            j = block_of(near, far, blocks)
            picked = []
            for slot in range(slots):
                row = rows_ref[slot, j]
                place = lax.rem(row // 2, 4)
                nodes = pl.ds(pl.multiple_of((row // 8) * side, side), side)
                use_own = lax.rem(row + rep, 2) == 0
                block = jnp.where(use_own, own_ref[place, nodes], other_ref[place, nodes])
                picked.append(jnp.where(slot < counts_ref[j], block, jnp.zeros_like(block)))
            term = matmul(jnp.concatenate(picked, axis=1), tiles_ref[j].reshape(slots * side, side))
            outgoing_ref[near, far * side : (far + 1) * side] = term.astype(BF16)
        outgoing_ref[near, fars * side :] = carried


def relay_terms(arrived_ref, outgoing_ref):
    nears, _, side = arrived_ref.shape
    fars = outgoing_ref.shape[0]
    total = arrived_ref[0].astype(F32)
    for k in range(1, nears):
        total += arrived_ref[k].astype(F32)
    total = total.astype(BF16)
    for g in range(fars):
        outgoing_ref[g, :side] = total[g * side : (g + 1) * side]
        outgoing_ref[g, side:] = total[fars * side :]


def final_sums(parts_ref, feature_grad_ref, weight_ref):
    fars, _, side = parts_ref.shape
    total = parts_ref[0].astype(F32)
    for k in range(1, fars):
        total += parts_ref[k].astype(F32)
    feature_grad_ref[...] = total[:side].T.astype(BF16)
    for x in range(weight_ref.shape[0]):
        weight_ref[x] = total[side:]


def call(kernel, inputs, outputs, scratch=()):
    return pl.pallas_call(
        kernel,
        out_shape=outputs,
        in_specs=inputs,
        out_specs=[VMEM] * len(outputs),
        scratch_shapes=scratch,
        compiler_params=pltpu.CompilerParams(vmem_limit_bytes=32 * 2**20),
    )


def local(blocks, replicas, features, weight, cotangent, tile_vals, tile_row, tile_count):
    def shape(*dims, dtype=BF16):
        return jax.ShapeDtypeStruct(dims, dtype)

    side, width = features.shape
    hidden = weight.shape[1]
    nears, fars = 4, blocks // 4
    x_fars, x_size = replicas // 8, replicas // 4
    lines = weight.size // x_size // side
    tiles, rows, counts = tile_vals[0, 0], tile_row[0, 0].T, tile_count[0, 0]

    near_blocks = [[block_of(k, g, blocks) for k in range(nears)] for g in range(fars)]
    far_blocks = [[block_of(k, g, blocks) for g in range(fars)] for k in range(nears)]
    near_rep = [[8 * f + 2 * k + c for k in range(4)] for f in range(x_fars) for c in range(2)]
    far_rep = [[8 * f + k for f in range(x_fars)] for k in range(8)]
    along_x = [[4 * x + k for x in range(x_size)] for k in range(4)]
    swap = [(r, r ^ 1) for r in range(replicas)]

    def exchange(block, axis, index_groups):
        return lax.all_to_all(block, axis, 0, 0, axis_index_groups=index_groups, tiled=True)

    with jax.named_scope("gather_features"):
        (copies,) = call(spread, [VMEM], [shape(fars, side, width)])(features)
        band = exchange(copies, "blk", far_blocks)
        (copies,) = call(spread, [VMEM], [shape(nears, fars, side, width)])(band)
        gathered = exchange(copies, "blk", near_blocks)
    kept, sent = call(
        forward_tiles,
        [SMEM, SMEM, VMEM, VMEM],
        [shape(4, x_fars, side, width, dtype=F32), shape(4, x_fars, side, width)],
        [pltpu.VMEM((2, 4, x_fars, side, width), F32)],
    )(rows, counts, gathered, tiles)
    with jax.named_scope("sum_partials"):
        pair = (kept + lax.ppermute(sent, "rep", swap).astype(F32)).astype(BF16)
        near_sum = jnp.sum(exchange(pair, "rep", near_rep).astype(F32), axis=0).astype(BF16)
        parts = exchange(near_sum, "rep", far_rep)
    activations, outgoing = call(
        dense_layer,
        [VMEM] * 3,
        [shape(side, hidden), shape(x_fars, side + 2 * lines, width)],
    )(parts, weight, cotangent)
    with jax.named_scope("gather_grads"):
        arrived = exchange(outgoing, "rep", far_rep)
        (outgoing,) = call(relay_grads, [VMEM], [shape(4, x_fars * side + lines, width)])(arrived)
        own = exchange(outgoing, "rep", near_rep)
        other = lax.ppermute(own, "rep", swap)
    (terms,) = call(
        backward_tiles,
        [SMEM, SMEM, VMEM, VMEM, VMEM],
        [shape(nears, fars * side + lines, width)],
    )(rows, counts, own, other, tiles)
    with jax.named_scope("sum_terms"):
        arrived = exchange(terms, "blk", near_blocks)
        (terms,) = call(relay_terms, [VMEM], [shape(fars, side + lines, width)])(arrived)
        arrived = exchange(terms, "blk", far_blocks)
    feature_grad, piece = call(
        final_sums,
        [VMEM],
        [shape(side, width), shape(x_size, lines, width, dtype=F32)],
    )(arrived)
    with jax.named_scope("gather_weight_grad"):
        pieces = exchange(piece, "rep", along_x).reshape(-1, hidden // side, 8, side)
    weight_grad = pieces.transpose(0, 2, 1, 3).reshape(weight.shape)
    return activations, feature_grad, weight_grad


def solution(mesh):
    in_specs = (
        P(("blk", "rep"), None),
        P(),
        P(("blk", "rep"), None),
        P("blk", "rep", None, None, None, None),
        P("blk", "rep", None, None),
        P("blk", "rep", None),
    )
    out_specs = (P(("blk", "rep"), None), P(("blk", "rep"), None), P())
    step = functools.partial(local, mesh.shape["blk"], mesh.shape["rep"])
    return jax.shard_map(step, mesh=mesh, in_specs=in_specs, out_specs=out_specs, check_vma=False)
```

```python
import functools

import jax
import jax.numpy as jnp
from jax import lax
from jax.experimental import pallas as pl
from jax.experimental.pallas import tpu as pltpu
from jax.sharding import PartitionSpec as P

VMEM = pl.BlockSpec(memory_space=pltpu.VMEM)
SMEM = pl.BlockSpec(memory_space=pltpu.SMEM)
F32 = jnp.float32
BF16 = jnp.bfloat16


def block_of(near, far, blocks):
    y_near, z_near = divmod(near, 2)
    y_far, z_far = divmod(far, blocks // 8)
    return ((y_far * 2 + y_near) * (blocks // 8) + z_far) * 2 + z_near


def matmul(a, b):
    return jnp.dot(a, b, preferred_element_type=F32)


def spread(block_ref, copies_ref):
    for k in range(copies_ref.shape[0]):
        copies_ref[k] = block_ref[...]


def forward_tiles(rows_ref, counts_ref, features_ref, tiles_ref, kept_ref, sent_ref, total):
    rep = lax.axis_index("rep")
    blocks, slots, side, _ = tiles_ref.shape
    total[...] = jnp.zeros_like(total)
    for near in range(features_ref.shape[0]):
        for far in range(features_ref.shape[1]):
            j = block_of(near, far, blocks)
            product = matmul(tiles_ref[j].reshape(slots * side, side), features_ref[near, far])
            for slot in range(slots):
                row = rows_ref[slot, j]
                term = product[slot * side : (slot + 1) * side]
                total[lax.rem(row + rep, 2), row // 2] += jnp.where(slot < counts_ref[j], term, 0.0)
    kept_ref[...] = total[0]
    sent_ref[...] = total[1].astype(sent_ref.dtype)


def sum_parts(parts_ref, copies_ref):
    for place in range(2):
        total = parts_ref[place].astype(F32)
        for g in range(place + 2, parts_ref.shape[0], 2):
            total += parts_ref[g].astype(F32)
        copies_ref[place] = total.astype(BF16)
        copies_ref[place + 2] = total.astype(BF16)


def dense_layer(
    halves_ref, weight_ref, cotangent_ref, partner_ref, activations_ref, outgoing_ref
):
    side = cotangent_ref.shape[0]
    first = lax.rem(lax.axis_index("rep") // 2, 2) == 0
    aggregated = jnp.concatenate(
        [halves_ref[k].astype(F32) + halves_ref[k + 2].astype(F32) for k in range(2)], axis=0
    ).astype(BF16)
    cotangent, partner = cotangent_ref[...].astype(F32), partner_ref[...].astype(F32)
    cotangent = jnp.concatenate(
        [jnp.where(first, cotangent, partner), jnp.where(first, partner, cotangent)], axis=0
    )
    weight = weight_ref[...]
    pre = matmul(aggregated, weight)
    sigma = jax.nn.sigmoid(pre)
    activations = pre * sigma
    activations_ref[...] = jnp.where(first, activations[:side], activations[side:]).astype(BF16)
    grad_pre = (cotangent * sigma * (1.0 + pre * (1.0 - sigma))).astype(BF16)
    grad_agg = lax.dot_general(
        weight, grad_pre, (((1,), (1,)), ((), ())), preferred_element_type=F32
    ).astype(BF16)
    term = lax.dot_general(
        aggregated, grad_pre, (((0,), (0,)), ((), ())), preferred_element_type=F32
    )
    pieces = [
        term[top : top + 8, left : left + side]
        for top in range(0, term.shape[0], 8)
        for left in range(0, term.shape[1], side)
    ]
    count = len(pieces) // outgoing_ref.shape[0]
    for x in range(outgoing_ref.shape[0]):
        outgoing_ref[x, :side] = grad_agg[:, :side]
        outgoing_ref[x, side : 2 * side] = grad_agg[:, side:]
        lines = jnp.concatenate(pieces[x * count : (x + 1) * count], axis=0)
        outgoing_ref[x, 2 * side :] = lines.astype(BF16)


def backward_tiles(rows_ref, counts_ref, own_ref, other_ref, tiles_ref, outgoing_ref):
    rep = lax.axis_index("rep")
    blocks, slots, side, _ = tiles_ref.shape
    nears = outgoing_ref.shape[0]
    fars = blocks // nears
    grads = 2 * side
    own_sum, other_sum = own_ref[0, grads:].astype(F32), other_ref[0, grads:].astype(F32)
    for x in range(1, own_ref.shape[0]):
        own_sum += own_ref[x, grads:].astype(F32)
        other_sum += other_ref[x, grads:].astype(F32)
    carried = (own_sum + other_sum).astype(BF16)
    for near in range(nears):
        for far in range(fars):
            j = block_of(near, far, blocks)
            picked = []
            for slot in range(slots):
                row = rows_ref[slot, j]
                x = row // 4
                nodes = pl.ds(pl.multiple_of(lax.rem(row // 2, 2) * side, side), side)
                use_own = lax.rem(row + rep, 2) == 0
                block = jnp.where(use_own, own_ref[x, nodes], other_ref[x, nodes])
                picked.append(jnp.where(slot < counts_ref[j], block, jnp.zeros_like(block)))
            term = matmul(jnp.concatenate(picked, axis=1), tiles_ref[j].reshape(slots * side, side))
            outgoing_ref[near, far * side : (far + 1) * side] = term.astype(BF16)
        outgoing_ref[near, fars * side :] = carried


def relay_terms(arrived_ref, outgoing_ref):
    nears, _, side = arrived_ref.shape
    fars = outgoing_ref.shape[0]
    total = arrived_ref[0].astype(F32)
    for k in range(1, nears):
        total += arrived_ref[k].astype(F32)
    total = total.astype(BF16)
    for g in range(fars):
        outgoing_ref[g, :side] = total[g * side : (g + 1) * side]
        outgoing_ref[g, side:] = total[fars * side :]


def final_sums(parts_ref, feature_grad_ref, weight_ref):
    fars, _, side = parts_ref.shape
    total = parts_ref[0].astype(F32)
    for k in range(1, fars):
        total += parts_ref[k].astype(F32)
    feature_grad_ref[...] = total[:side].T.astype(BF16)
    for x in range(weight_ref.shape[0]):
        weight_ref[x] = total[side:]


def call(kernel, inputs, outputs, scratch=()):
    return pl.pallas_call(
        kernel,
        out_shape=outputs,
        in_specs=inputs,
        out_specs=[VMEM] * len(outputs),
        scratch_shapes=scratch,
        compiler_params=pltpu.CompilerParams(vmem_limit_bytes=32 * 2**20),
    )


def local(blocks, replicas, features, weight, cotangent, tile_vals, tile_row, tile_count):
    def shape(*dims, dtype=BF16):
        return jax.ShapeDtypeStruct(dims, dtype)

    side, width = features.shape
    hidden = weight.shape[1]
    nears, fars = 4, blocks // 4
    groups, x_size = replicas // 2, replicas // 4
    lines = weight.size // x_size // side
    tiles, rows, counts = tile_vals[0, 0], tile_row[0, 0].T, tile_count[0, 0]

    near_blocks = [[block_of(k, g, blocks) for k in range(nears)] for g in range(fars)]
    far_blocks = [[block_of(k, g, blocks) for g in range(fars)] for k in range(nears)]
    y_pairs = [[4 * x + c, 4 * x + 2 + c] for x in range(x_size) for c in range(2)]
    along_x = [[4 * x + k for x in range(x_size)] for k in range(4)]
    swap = [(r, r ^ 1) for r in range(replicas)]
    swap_y = [(r, r ^ 2) for r in range(replicas)]

    def exchange(block, axis, index_groups):
        return lax.all_to_all(block, axis, 0, 0, axis_index_groups=index_groups, tiled=True)

    with jax.named_scope("partner_cotangent"):
        partner = lax.ppermute(cotangent, "rep", swap_y)
    with jax.named_scope("gather_features"):
        (copies,) = call(spread, [VMEM], [shape(fars, side, width)])(features)
        band = exchange(copies, "blk", far_blocks)
        (copies,) = call(spread, [VMEM], [shape(nears, fars, side, width)])(band)
        gathered = exchange(copies, "blk", near_blocks)
    kept, sent = call(
        forward_tiles,
        [SMEM, SMEM, VMEM, VMEM],
        [shape(groups, side, width, dtype=F32), shape(groups, side, width)],
        [pltpu.VMEM((2, groups, side, width), F32)],
    )(rows, counts, gathered, tiles)
    with jax.named_scope("sum_partials"):
        pair = (kept + lax.ppermute(sent, "rep", swap).astype(F32)).astype(BF16)
        parts = exchange(pair, "rep", along_x)
        (copies,) = call(sum_parts, [VMEM], [shape(4, side, width)])(parts)
        halves = exchange(copies, "rep", y_pairs)
    activations, outgoing = call(
        dense_layer,
        [VMEM] * 4,
        [shape(side, hidden), shape(x_size, 2 * side + lines, width)],
    )(halves, weight, cotangent, partner)
    with jax.named_scope("gather_grads"):
        own = exchange(outgoing, "rep", along_x)
        other = lax.ppermute(own, "rep", swap)
    (terms,) = call(
        backward_tiles,
        [SMEM, SMEM, VMEM, VMEM, VMEM],
        [shape(nears, fars * side + lines, width)],
    )(rows, counts, own, other, tiles)
    with jax.named_scope("sum_terms"):
        arrived = exchange(terms, "blk", near_blocks)
        (terms,) = call(relay_terms, [VMEM], [shape(fars, side + lines, width)])(arrived)
        arrived = exchange(terms, "blk", far_blocks)
    feature_grad, piece = call(
        final_sums,
        [VMEM],
        [shape(side, width), shape(x_size, lines, width, dtype=F32)],
    )(arrived)
    with jax.named_scope("gather_weight_grad"):
        pieces = exchange(piece, "rep", along_x).reshape(-1, hidden // side, 8, side)
    weight_grad = pieces.transpose(0, 2, 1, 3).reshape(weight.shape)
    return activations, feature_grad, weight_grad


def solution(mesh):
    in_specs = (
        P(("blk", "rep"), None),
        P(),
        P(("blk", "rep"), None),
        P("blk", "rep", None, None, None, None),
        P("blk", "rep", None, None),
        P("blk", "rep", None),
    )
    out_specs = (P(("blk", "rep"), None), P(("blk", "rep"), None), P())
    step = functools.partial(local, mesh.shape["blk"], mesh.shape["rep"])
    return jax.shard_map(step, mesh=mesh, in_specs=in_specs, out_specs=out_specs, check_vma=False)
```

```python
import functools

import jax
import jax.numpy as jnp
from jax import lax
from jax.experimental import pallas as pl
from jax.experimental.pallas import tpu as pltpu
from jax.sharding import PartitionSpec as P

VMEM = pl.BlockSpec(memory_space=pltpu.VMEM)
SMEM = pl.BlockSpec(memory_space=pltpu.SMEM)
F32 = jnp.float32
BF16 = jnp.bfloat16


def block_of(near, far, blocks):
    y_near, z_near = divmod(near, 2)
    y_far, z_far = divmod(far, blocks // 8)
    return ((y_far * 2 + y_near) * (blocks // 8) + z_far) * 2 + z_near


def matmul(a, b):
    return jnp.dot(a, b, preferred_element_type=F32)


def spread(block_ref, copies_ref):
    for k in range(copies_ref.shape[0]):
        copies_ref[k] = block_ref[...]


def forward_tiles(rows_ref, counts_ref, features_ref, tiles_ref, kept_ref, sent_ref, total):
    rep = lax.axis_index("rep")
    blocks, slots, side, _ = tiles_ref.shape
    total[...] = jnp.zeros_like(total)
    for near in range(features_ref.shape[0]):
        for far in range(features_ref.shape[1]):
            j = block_of(near, far, blocks)
            product = matmul(tiles_ref[j].reshape(slots * side, side), features_ref[near, far])
            for slot in range(slots):
                row = rows_ref[slot, j]
                term = product[slot * side : (slot + 1) * side]
                total[lax.rem(row + rep, 2), row // 2] += jnp.where(slot < counts_ref[j], term, 0.0)
    kept_ref[...] = total[0]
    sent_ref[...] = total[1].astype(sent_ref.dtype)


def sum_parts(parts_ref, copies_ref):
    for place in range(2):
        total = parts_ref[place].astype(F32)
        for g in range(place + 2, parts_ref.shape[0], 2):
            total += parts_ref[g].astype(F32)
        copies_ref[place] = total.astype(BF16)
        copies_ref[place + 2] = total.astype(BF16)


def dense_layer(
    halves_ref, weight_ref, cotangent_ref, partner_ref, activations_ref, outgoing_ref
):
    side = cotangent_ref.shape[0]
    first = lax.rem(lax.axis_index("rep") // 2, 2) == 0
    aggregated = jnp.concatenate(
        [halves_ref[k].astype(F32) + halves_ref[k + 2].astype(F32) for k in range(2)], axis=0
    ).astype(BF16)
    cotangent, partner = cotangent_ref[...].astype(F32), partner_ref[...].astype(F32)
    cotangent = jnp.concatenate(
        [jnp.where(first, cotangent, partner), jnp.where(first, partner, cotangent)], axis=0
    )
    weight = weight_ref[...]
    pre = matmul(aggregated, weight)
    sigma = jax.nn.sigmoid(pre)
    activations = pre * sigma
    activations_ref[...] = jnp.where(first, activations[:side], activations[side:]).astype(BF16)
    grad_pre = (cotangent * sigma * (1.0 + pre * (1.0 - sigma))).astype(BF16)
    grad_agg = lax.dot_general(
        weight, grad_pre, (((1,), (1,)), ((), ())), preferred_element_type=F32
    ).astype(BF16)
    term = lax.dot_general(
        aggregated, grad_pre, (((0,), (0,)), ((), ())), preferred_element_type=F32
    )
    pieces = [
        term[top : top + 8, left : left + side]
        for top in range(0, term.shape[0], 8)
        for left in range(0, term.shape[1], side)
    ]
    count = len(pieces) // outgoing_ref.shape[0]
    for x in range(outgoing_ref.shape[0]):
        outgoing_ref[x, :side] = grad_agg[:, :side]
        outgoing_ref[x, side : 2 * side] = grad_agg[:, side:]
        lines = jnp.concatenate(pieces[x * count : (x + 1) * count], axis=0)
        outgoing_ref[x, 2 * side :] = lines.astype(BF16)


def backward_tiles(rows_ref, counts_ref, own_ref, other_ref, tiles_ref, outgoing_ref):
    rep = lax.axis_index("rep")
    blocks, slots, side, _ = tiles_ref.shape
    nears = outgoing_ref.shape[0]
    fars = blocks // nears
    grads = 2 * side
    own_sum, other_sum = own_ref[0, grads:].astype(F32), other_ref[0, grads:].astype(F32)
    for x in range(1, own_ref.shape[0]):
        own_sum += own_ref[x, grads:].astype(F32)
        other_sum += other_ref[x, grads:].astype(F32)
    carried = (own_sum + other_sum).astype(BF16)
    for near in range(nears):
        for far in range(fars):
            j = block_of(near, far, blocks)
            picked = []
            for slot in range(slots):
                row = rows_ref[slot, j]
                x = row // 4
                nodes = pl.ds(pl.multiple_of(lax.rem(row // 2, 2) * side, side), side)
                use_own = lax.rem(row + rep, 2) == 0
                block = jnp.where(use_own, own_ref[x, nodes], other_ref[x, nodes])
                picked.append(jnp.where(slot < counts_ref[j], block, jnp.zeros_like(block)))
            term = matmul(jnp.concatenate(picked, axis=1), tiles_ref[j].reshape(slots * side, side))
            outgoing_ref[near, far * side : (far + 1) * side] = term.astype(BF16)
        outgoing_ref[near, fars * side :] = carried


def relay_terms(arrived_ref, outgoing_ref):
    nears, _, side = arrived_ref.shape
    fars = outgoing_ref.shape[0]
    total = arrived_ref[0].astype(F32)
    for k in range(1, nears):
        total += arrived_ref[k].astype(F32)
    total = total.astype(BF16)
    for g in range(fars):
        outgoing_ref[g, :side] = total[g * side : (g + 1) * side]
        outgoing_ref[g, side:] = total[fars * side :]


def final_sums(parts_ref, feature_grad_ref, weight_ref):
    fars, _, side = parts_ref.shape
    total = parts_ref[0].astype(F32)
    for k in range(1, fars):
        total += parts_ref[k].astype(F32)
    feature_grad_ref[...] = total[:side].T.astype(BF16)
    for x in range(weight_ref.shape[0]):
        weight_ref[x] = total[side:]


def call(kernel, inputs, outputs, scratch=()):
    return pl.pallas_call(
        kernel,
        out_shape=outputs,
        in_specs=inputs,
        out_specs=[VMEM] * len(outputs),
        scratch_shapes=scratch,
        compiler_params=pltpu.CompilerParams(vmem_limit_bytes=32 * 2**20),
    )


def local(blocks, replicas, features, weight, cotangent, tile_vals, tile_row, tile_count):
    def shape(*dims, dtype=BF16):
        return jax.ShapeDtypeStruct(dims, dtype)

    side, width = features.shape
    hidden = weight.shape[1]
    nears, fars = 4, blocks // 4
    groups, x_size = replicas // 2, replicas // 4
    lines = weight.size // x_size // side
    tiles, rows, counts = tile_vals[0, 0], tile_row[0, 0].T, tile_count[0, 0]

    near_blocks = [[block_of(k, g, blocks) for k in range(nears)] for g in range(fars)]
    far_blocks = [[block_of(k, g, blocks) for g in range(fars)] for k in range(nears)]
    y_pairs = [[4 * x + c, 4 * x + 2 + c] for x in range(x_size) for c in range(2)]
    along_x = [[4 * x + k for x in range(x_size)] for k in range(4)]
    swap = [(r, r ^ 1) for r in range(replicas)]
    swap_y = [(r, r ^ 2) for r in range(replicas)]

    def exchange(block, axis, index_groups):
        return lax.all_to_all(block, axis, 0, 0, axis_index_groups=index_groups, tiled=True)

    with jax.named_scope("partner_cotangent"):
        partner = lax.ppermute(cotangent, "rep", swap_y)
    with jax.named_scope("gather_features"):
        (copies,) = call(spread, [VMEM], [shape(fars, side, width)])(features)
        band = exchange(copies, "blk", far_blocks)
        (copies,) = call(spread, [VMEM], [shape(nears, fars, side, width)])(band)
        gathered = exchange(copies, "blk", near_blocks)
        gathered, partner = lax.optimization_barrier((gathered, partner))
    kept, sent = call(
        forward_tiles,
        [SMEM, SMEM, VMEM, VMEM],
        [shape(groups, side, width, dtype=F32), shape(groups, side, width)],
        [pltpu.VMEM((2, groups, side, width), F32)],
    )(rows, counts, gathered, tiles)
    with jax.named_scope("sum_partials"):
        pair = (kept + lax.ppermute(sent, "rep", swap).astype(F32)).astype(BF16)
        parts = exchange(pair, "rep", along_x)
        (copies,) = call(sum_parts, [VMEM], [shape(4, side, width)])(parts)
        halves = exchange(copies, "rep", y_pairs)
    activations, outgoing = call(
        dense_layer,
        [VMEM] * 4,
        [shape(side, hidden), shape(x_size, 2 * side + lines, width)],
    )(halves, weight, cotangent, partner)
    with jax.named_scope("gather_grads"):
        own = exchange(outgoing, "rep", along_x)
        other = lax.ppermute(own, "rep", swap)
    (terms,) = call(
        backward_tiles,
        [SMEM, SMEM, VMEM, VMEM, VMEM],
        [shape(nears, fars * side + lines, width)],
    )(rows, counts, own, other, tiles)
    with jax.named_scope("sum_terms"):
        arrived = exchange(terms, "blk", near_blocks)
        (terms,) = call(relay_terms, [VMEM], [shape(fars, side + lines, width)])(arrived)
        arrived = exchange(terms, "blk", far_blocks)
    feature_grad, piece = call(
        final_sums,
        [VMEM],
        [shape(side, width), shape(x_size, lines, width, dtype=F32)],
    )(arrived)
    with jax.named_scope("gather_weight_grad"):
        pieces = exchange(piece, "rep", along_x).reshape(-1, hidden // side, 8, side)
    weight_grad = pieces.transpose(0, 2, 1, 3).reshape(weight.shape)
    return activations, feature_grad, weight_grad


def solution(mesh):
    in_specs = (
        P(("blk", "rep"), None),
        P(),
        P(("blk", "rep"), None),
        P("blk", "rep", None, None, None, None),
        P("blk", "rep", None, None),
        P("blk", "rep", None),
    )
    out_specs = (P(("blk", "rep"), None), P(("blk", "rep"), None), P())
    step = functools.partial(local, mesh.shape["blk"], mesh.shape["rep"])
    return jax.shard_map(step, mesh=mesh, in_specs=in_specs, out_specs=out_specs, check_vma=False)
```

```python
import functools

import jax
import jax.numpy as jnp
from jax import lax
from jax.experimental import pallas as pl
from jax.experimental.pallas import tpu as pltpu
from jax.sharding import PartitionSpec as P

VMEM = pl.BlockSpec(memory_space=pltpu.VMEM)
SMEM = pl.BlockSpec(memory_space=pltpu.SMEM)
F32 = jnp.float32
BF16 = jnp.bfloat16


def block_of(near, far, blocks):
    y_near, z_near = divmod(near, 2)
    y_far, z_far = divmod(far, blocks // 8)
    return ((y_far * 2 + y_near) * (blocks // 8) + z_far) * 2 + z_near


def matmul(a, b):
    return jnp.dot(a, b, preferred_element_type=F32)


def spread(block_ref, copies_ref):
    for k in range(copies_ref.shape[0]):
        copies_ref[k] = block_ref[...]


def forward_tiles(rows_ref, counts_ref, features_ref, tiles_ref, kept_ref, sent_ref, total):
    rep = lax.axis_index("rep")
    blocks, slots, side, _ = tiles_ref.shape
    total[...] = jnp.zeros_like(total)
    for near in range(features_ref.shape[0]):
        for far in range(features_ref.shape[1]):
            j = block_of(near, far, blocks)
            product = matmul(tiles_ref[j].reshape(slots * side, side), features_ref[near, far])
            for slot in range(slots):
                row = rows_ref[slot, j]
                term = product[slot * side : (slot + 1) * side]
                total[lax.rem(row + rep, 2), row // 2] += jnp.where(slot < counts_ref[j], term, 0.0)
    kept_ref[...] = total[0]
    sent_ref[...] = total[1].astype(sent_ref.dtype)


def sum_parts(parts_ref, copies_ref):
    for place in range(2):
        total = parts_ref[place].astype(F32)
        for g in range(place + 2, parts_ref.shape[0], 2):
            total += parts_ref[g].astype(F32)
        copies_ref[place] = total.astype(BF16)
        copies_ref[place + 2] = total.astype(BF16)


def dense_layer(
    halves_ref, weight_ref, cotangent_ref, partner_ref, activations_ref, outgoing_ref
):
    side = cotangent_ref.shape[0]
    first = lax.rem(lax.axis_index("rep") // 2, 2) == 0
    aggregated = jnp.concatenate(
        [halves_ref[k].astype(F32) + halves_ref[k + 2].astype(F32) for k in range(2)], axis=0
    ).astype(BF16)
    cotangent, partner = cotangent_ref[...].astype(F32), partner_ref[...].astype(F32)
    cotangent = jnp.concatenate(
        [jnp.where(first, cotangent, partner), jnp.where(first, partner, cotangent)], axis=0
    )
    weight = weight_ref[...]
    pre = matmul(aggregated, weight)
    sigma = jax.nn.sigmoid(pre)
    activations = pre * sigma
    activations_ref[...] = jnp.where(first, activations[:side], activations[side:]).astype(BF16)
    grad_pre = (cotangent * sigma * (1.0 + pre * (1.0 - sigma))).astype(BF16)
    grad_agg = lax.dot_general(
        weight, grad_pre, (((1,), (1,)), ((), ())), preferred_element_type=F32
    ).astype(BF16)
    term = lax.dot_general(
        aggregated, grad_pre, (((0,), (0,)), ((), ())), preferred_element_type=F32
    )
    pieces = [
        term[top : top + 8, left : left + side]
        for top in range(0, term.shape[0], 8)
        for left in range(0, term.shape[1], side)
    ]
    count = len(pieces) // outgoing_ref.shape[0]
    for x in range(outgoing_ref.shape[0]):
        outgoing_ref[x, :side] = grad_agg[:, :side]
        outgoing_ref[x, side : 2 * side] = grad_agg[:, side:]
        lines = jnp.concatenate(pieces[x * count : (x + 1) * count], axis=0)
        outgoing_ref[x, 2 * side :] = lines.astype(BF16)


def backward_tiles(rows_ref, counts_ref, own_ref, other_ref, tiles_ref, outgoing_ref):
    rep = lax.axis_index("rep")
    blocks, slots, side, _ = tiles_ref.shape
    nears = outgoing_ref.shape[0]
    fars = blocks // nears
    grads = 2 * side
    own_sum, other_sum = own_ref[0, grads:].astype(F32), other_ref[0, grads:].astype(F32)
    for x in range(1, own_ref.shape[0]):
        own_sum += own_ref[x, grads:].astype(F32)
        other_sum += other_ref[x, grads:].astype(F32)
    carried = (own_sum + other_sum).astype(BF16)
    for near in range(nears):
        for far in range(fars):
            j = block_of(near, far, blocks)
            picked = []
            for slot in range(slots):
                row = rows_ref[slot, j]
                x = row // 4
                nodes = pl.ds(pl.multiple_of(lax.rem(row // 2, 2) * side, side), side)
                use_own = lax.rem(row + rep, 2) == 0
                block = jnp.where(use_own, own_ref[x, nodes], other_ref[x, nodes])
                picked.append(jnp.where(slot < counts_ref[j], block, jnp.zeros_like(block)))
            term = matmul(jnp.concatenate(picked, axis=1), tiles_ref[j].reshape(slots * side, side))
            outgoing_ref[near, far * side : (far + 1) * side] = term.astype(BF16)
        outgoing_ref[near, fars * side :] = carried


def relay_terms(arrived_ref, outgoing_ref):
    nears, _, side = arrived_ref.shape
    fars = outgoing_ref.shape[0]
    total = arrived_ref[0].astype(F32)
    for k in range(1, nears):
        total += arrived_ref[k].astype(F32)
    total = total.astype(BF16)
    for g in range(fars):
        outgoing_ref[g, :side] = total[g * side : (g + 1) * side]
        outgoing_ref[g, side:] = total[fars * side :]


def final_sums(parts_ref, feature_grad_ref, weight_ref):
    fars, _, side = parts_ref.shape
    total = parts_ref[0].astype(F32)
    for k in range(1, fars):
        total += parts_ref[k].astype(F32)
    feature_grad_ref[...] = total[:side].T.astype(BF16)
    for x in range(weight_ref.shape[0]):
        weight_ref[x] = total[side:]


def call(kernel, inputs, outputs, scratch=()):
    return pl.pallas_call(
        kernel,
        out_shape=outputs,
        in_specs=inputs,
        out_specs=[VMEM] * len(outputs),
        scratch_shapes=scratch,
        compiler_params=pltpu.CompilerParams(vmem_limit_bytes=32 * 2**20),
    )


def local(blocks, replicas, features, weight, cotangent, tile_vals, tile_row, tile_count):
    def shape(*dims, dtype=BF16):
        return jax.ShapeDtypeStruct(dims, dtype)

    side, width = features.shape
    hidden = weight.shape[1]
    nears, fars = 4, blocks // 4
    groups, x_size = replicas // 2, replicas // 4
    lines = weight.size // x_size // side
    tiles, rows, counts = tile_vals[0, 0], tile_row[0, 0].T, tile_count[0, 0]

    near_blocks = [[block_of(k, g, blocks) for k in range(nears)] for g in range(fars)]
    far_blocks = [[block_of(k, g, blocks) for g in range(fars)] for k in range(nears)]
    y_pairs = [[4 * x + c, 4 * x + 2 + c] for x in range(x_size) for c in range(2)]
    along_x = [[4 * x + k for x in range(x_size)] for k in range(4)]
    swap = [(r, r ^ 1) for r in range(replicas)]
    swap_y = [(r, r ^ 2) for r in range(replicas)]

    def exchange(block, axis, index_groups):
        return lax.all_to_all(block, axis, 0, 0, axis_index_groups=index_groups, tiled=True)

    with jax.named_scope("gather_features"):
        (copies,) = call(spread, [VMEM], [shape(fars, side, width)])(features)
        band = exchange(copies, "blk", far_blocks)
        (copies,) = call(spread, [VMEM], [shape(nears, fars, side, width)])(band)
        gathered = exchange(copies, "blk", near_blocks)
    kept, sent = call(
        forward_tiles,
        [SMEM, SMEM, VMEM, VMEM],
        [shape(groups, side, width, dtype=F32), shape(groups, side, width)],
        [pltpu.VMEM((2, groups, side, width), F32)],
    )(rows, counts, gathered, tiles)
    with jax.named_scope("sum_partials"):
        pair = (kept + lax.ppermute(sent, "rep", swap).astype(F32)).astype(BF16)
        pair, lent = lax.optimization_barrier((pair, cotangent))
        parts = exchange(pair, "rep", along_x)
        partner = lax.ppermute(lent, "rep", swap_y)
        parts, partner = lax.optimization_barrier((parts, partner))
        (copies,) = call(sum_parts, [VMEM], [shape(4, side, width)])(parts)
        halves = exchange(copies, "rep", y_pairs)
    activations, outgoing = call(
        dense_layer,
        [VMEM] * 4,
        [shape(side, hidden), shape(x_size, 2 * side + lines, width)],
    )(halves, weight, cotangent, partner)
    with jax.named_scope("gather_grads"):
        own = exchange(outgoing, "rep", along_x)
        other = lax.ppermute(own, "rep", swap)
    (terms,) = call(
        backward_tiles,
        [SMEM, SMEM, VMEM, VMEM, VMEM],
        [shape(nears, fars * side + lines, width)],
    )(rows, counts, own, other, tiles)
    with jax.named_scope("sum_terms"):
        arrived = exchange(terms, "blk", near_blocks)
        (terms,) = call(relay_terms, [VMEM], [shape(fars, side + lines, width)])(arrived)
        arrived = exchange(terms, "blk", far_blocks)
    feature_grad, piece = call(
        final_sums,
        [VMEM],
        [shape(side, width), shape(x_size, lines, width, dtype=F32)],
    )(arrived)
    with jax.named_scope("gather_weight_grad"):
        pieces = exchange(piece, "rep", along_x).reshape(-1, hidden // side, 8, side)
    weight_grad = pieces.transpose(0, 2, 1, 3).reshape(weight.shape)
    return activations, feature_grad, weight_grad


def solution(mesh):
    in_specs = (
        P(("blk", "rep"), None),
        P(),
        P(("blk", "rep"), None),
        P("blk", "rep", None, None, None, None),
        P("blk", "rep", None, None),
        P("blk", "rep", None),
    )
    out_specs = (P(("blk", "rep"), None), P(("blk", "rep"), None), P())
    step = functools.partial(local, mesh.shape["blk"], mesh.shape["rep"])
    return jax.shard_map(step, mesh=mesh, in_specs=in_specs, out_specs=out_specs, check_vma=False)
```

```python
import functools

import jax
import jax.numpy as jnp
from jax import lax
from jax.experimental import pallas as pl
from jax.experimental.pallas import tpu as pltpu
from jax.sharding import PartitionSpec as P

VMEM = pl.BlockSpec(memory_space=pltpu.VMEM)
SMEM = pl.BlockSpec(memory_space=pltpu.SMEM)
F32 = jnp.float32
BF16 = jnp.bfloat16


def block_of(near, far, blocks):
    y_near, z_near = divmod(near, 2)
    y_far, z_far = divmod(far, blocks // 8)
    return ((y_far * 2 + y_near) * (blocks // 8) + z_far) * 2 + z_near


def matmul(a, b):
    return jnp.dot(a, b, preferred_element_type=F32)


def spread(block_ref, copies_ref):
    for k in range(copies_ref.shape[0]):
        copies_ref[k] = block_ref[...]


def forward_tiles(rows_ref, counts_ref, features_ref, tiles_ref, kept_ref, sent_ref, total):
    rep = lax.axis_index("rep")
    blocks, slots, side, _ = tiles_ref.shape
    total[...] = jnp.zeros_like(total)
    for near in range(features_ref.shape[0]):
        for far in range(features_ref.shape[1]):
            j = block_of(near, far, blocks)
            product = matmul(tiles_ref[j].reshape(slots * side, side), features_ref[near, far])
            for slot in range(slots):
                row = rows_ref[slot, j]
                term = product[slot * side : (slot + 1) * side]
                total[lax.rem(row + rep, 2), row // 2] += jnp.where(slot < counts_ref[j], term, 0.0)
    kept_ref[...] = total[0]
    sent_ref[...] = total[1].astype(sent_ref.dtype)


def sum_parts(parts_ref, cotangent_ref, copies_ref):
    side = parts_ref.shape[1]
    for place in range(2):
        total = parts_ref[place].astype(F32)
        for g in range(place + 2, parts_ref.shape[0], 2):
            total += parts_ref[g].astype(F32)
        for partner in range(2):
            copies_ref[4 * partner + place] = total.astype(BF16)
            copies_ref[4 * partner + 2 + place] = cotangent_ref[:, place * side : (place + 1) * side]


def dense_layer(halves_ref, weight_ref, activations_ref, outgoing_ref):
    side = halves_ref.shape[1]
    first = lax.rem(lax.axis_index("rep") // 2, 2) == 0
    aggregated = jnp.concatenate(
        [halves_ref[k].astype(F32) + halves_ref[k + 4].astype(F32) for k in range(2)], axis=0
    ).astype(BF16)
    cotangent = jnp.concatenate(
        [jnp.concatenate([halves_ref[k + 2], halves_ref[k + 3]], axis=1) for k in (0, 4)], axis=0
    ).astype(F32)
    weight = weight_ref[...]
    pre = matmul(aggregated, weight)
    sigma = jax.nn.sigmoid(pre)
    activations = pre * sigma
    activations_ref[...] = jnp.where(first, activations[:side], activations[side:]).astype(BF16)
    grad_pre = (cotangent * sigma * (1.0 + pre * (1.0 - sigma))).astype(BF16)
    grad_agg = lax.dot_general(
        weight, grad_pre, (((1,), (1,)), ((), ())), preferred_element_type=F32
    ).astype(BF16)
    term = lax.dot_general(
        aggregated, grad_pre, (((0,), (0,)), ((), ())), preferred_element_type=F32
    )
    pieces = [
        term[top : top + 8, left : left + side]
        for top in range(0, term.shape[0], 8)
        for left in range(0, term.shape[1], side)
    ]
    count = len(pieces) // outgoing_ref.shape[0]
    for x in range(outgoing_ref.shape[0]):
        outgoing_ref[x, :side] = grad_agg[:, :side]
        outgoing_ref[x, side : 2 * side] = grad_agg[:, side:]
        lines = jnp.concatenate(pieces[x * count : (x + 1) * count], axis=0)
        outgoing_ref[x, 2 * side :] = lines.astype(BF16)


def backward_tiles(rows_ref, counts_ref, own_ref, other_ref, tiles_ref, outgoing_ref):
    rep = lax.axis_index("rep")
    blocks, slots, side, _ = tiles_ref.shape
    nears = outgoing_ref.shape[0]
    fars = blocks // nears
    grads = 2 * side
    own_sum, other_sum = own_ref[0, grads:].astype(F32), other_ref[0, grads:].astype(F32)
    for x in range(1, own_ref.shape[0]):
        own_sum += own_ref[x, grads:].astype(F32)
        other_sum += other_ref[x, grads:].astype(F32)
    carried = (own_sum + other_sum).astype(BF16)
    for near in range(nears):
        for far in range(fars):
            j = block_of(near, far, blocks)
            picked = []
            for slot in range(slots):
                row = rows_ref[slot, j]
                x = row // 4
                nodes = pl.ds(pl.multiple_of(lax.rem(row // 2, 2) * side, side), side)
                use_own = lax.rem(row + rep, 2) == 0
                block = jnp.where(use_own, own_ref[x, nodes], other_ref[x, nodes])
                picked.append(jnp.where(slot < counts_ref[j], block, jnp.zeros_like(block)))
            term = matmul(jnp.concatenate(picked, axis=1), tiles_ref[j].reshape(slots * side, side))
            outgoing_ref[near, far * side : (far + 1) * side] = term.astype(BF16)
        outgoing_ref[near, fars * side :] = carried


def relay_terms(arrived_ref, outgoing_ref):
    nears, _, side = arrived_ref.shape
    fars = outgoing_ref.shape[0]
    total = arrived_ref[0].astype(F32)
    for k in range(1, nears):
        total += arrived_ref[k].astype(F32)
    total = total.astype(BF16)
    for g in range(fars):
        outgoing_ref[g, :side] = total[g * side : (g + 1) * side]
        outgoing_ref[g, side:] = total[fars * side :]


def final_sums(parts_ref, feature_grad_ref, weight_ref):
    fars, _, side = parts_ref.shape
    total = parts_ref[0].astype(F32)
    for k in range(1, fars):
        total += parts_ref[k].astype(F32)
    feature_grad_ref[...] = total[:side].T.astype(BF16)
    for x in range(weight_ref.shape[0]):
        weight_ref[x] = total[side:]


def call(kernel, inputs, outputs, scratch=()):
    return pl.pallas_call(
        kernel,
        out_shape=outputs,
        in_specs=inputs,
        out_specs=[VMEM] * len(outputs),
        scratch_shapes=scratch,
        compiler_params=pltpu.CompilerParams(vmem_limit_bytes=32 * 2**20),
    )


def local(blocks, replicas, features, weight, cotangent, tile_vals, tile_row, tile_count):
    def shape(*dims, dtype=BF16):
        return jax.ShapeDtypeStruct(dims, dtype)

    side, width = features.shape
    hidden = weight.shape[1]
    nears, fars = 4, blocks // 4
    groups, x_size = replicas // 2, replicas // 4
    lines = weight.size // x_size // side
    tiles, rows, counts = tile_vals[0, 0], tile_row[0, 0].T, tile_count[0, 0]

    near_blocks = [[block_of(k, g, blocks) for k in range(nears)] for g in range(fars)]
    far_blocks = [[block_of(k, g, blocks) for g in range(fars)] for k in range(nears)]
    y_pairs = [[4 * x + c, 4 * x + 2 + c] for x in range(x_size) for c in range(2)]
    along_x = [[4 * x + k for x in range(x_size)] for k in range(4)]
    swap = [(r, r ^ 1) for r in range(replicas)]

    def exchange(block, axis, index_groups):
        return lax.all_to_all(block, axis, 0, 0, axis_index_groups=index_groups, tiled=True)

    with jax.named_scope("gather_features"):
        (copies,) = call(spread, [VMEM], [shape(fars, side, width)])(features)
        band = exchange(copies, "blk", far_blocks)
        (copies,) = call(spread, [VMEM], [shape(nears, fars, side, width)])(band)
        gathered = exchange(copies, "blk", near_blocks)
    kept, sent = call(
        forward_tiles,
        [SMEM, SMEM, VMEM, VMEM],
        [shape(groups, side, width, dtype=F32), shape(groups, side, width)],
        [pltpu.VMEM((2, groups, side, width), F32)],
    )(rows, counts, gathered, tiles)
    with jax.named_scope("sum_partials"):
        pair = (kept + lax.ppermute(sent, "rep", swap).astype(F32)).astype(BF16)
        parts = exchange(pair, "rep", along_x)
        (copies,) = call(sum_parts, [VMEM] * 2, [shape(8, side, width)])(parts, cotangent)
        halves = exchange(copies, "rep", y_pairs)
    activations, outgoing = call(
        dense_layer,
        [VMEM] * 2,
        [shape(side, hidden), shape(x_size, 2 * side + lines, width)],
    )(halves, weight)
    with jax.named_scope("gather_grads"):
        own = exchange(outgoing, "rep", along_x)
        other = lax.ppermute(own, "rep", swap)
    (terms,) = call(
        backward_tiles,
        [SMEM, SMEM, VMEM, VMEM, VMEM],
        [shape(nears, fars * side + lines, width)],
    )(rows, counts, own, other, tiles)
    with jax.named_scope("sum_terms"):
        arrived = exchange(terms, "blk", near_blocks)
        (terms,) = call(relay_terms, [VMEM], [shape(fars, side + lines, width)])(arrived)
        arrived = exchange(terms, "blk", far_blocks)
    feature_grad, piece = call(
        final_sums,
        [VMEM],
        [shape(side, width), shape(x_size, lines, width, dtype=F32)],
    )(arrived)
    with jax.named_scope("gather_weight_grad"):
        pieces = exchange(piece, "rep", along_x).reshape(-1, hidden // side, 8, side)
    weight_grad = pieces.transpose(0, 2, 1, 3).reshape(weight.shape)
    return activations, feature_grad, weight_grad


def solution(mesh):
    in_specs = (
        P(("blk", "rep"), None),
        P(),
        P(("blk", "rep"), None),
        P("blk", "rep", None, None, None, None),
        P("blk", "rep", None, None),
        P("blk", "rep", None),
    )
    out_specs = (P(("blk", "rep"), None), P(("blk", "rep"), None), P())
    step = functools.partial(local, mesh.shape["blk"], mesh.shape["rep"])
    return jax.shard_map(step, mesh=mesh, in_specs=in_specs, out_specs=out_specs, check_vma=False)
```

```python
import functools

import jax
import jax.numpy as jnp
from jax import lax
from jax.experimental import pallas as pl
from jax.experimental.pallas import tpu as pltpu
from jax.sharding import PartitionSpec as P

VMEM = pl.BlockSpec(memory_space=pltpu.VMEM)
SMEM = pl.BlockSpec(memory_space=pltpu.SMEM)
F32 = jnp.float32
BF16 = jnp.bfloat16


def block_of(near, far, blocks):
    y_near, z_near = divmod(near, 2)
    y_far, z_far = divmod(far, blocks // 8)
    return ((y_far * 2 + y_near) * (blocks // 8) + z_far) * 2 + z_near


def matmul(a, b):
    return jnp.dot(a, b, preferred_element_type=F32)


def spread(block_ref, copies_ref):
    for k in range(copies_ref.shape[0]):
        copies_ref[k] = block_ref[...]


def forward_tiles(rows_ref, counts_ref, features_ref, tiles_ref, kept_ref, sent_ref, total):
    rep = lax.axis_index("rep")
    blocks, slots, side, _ = tiles_ref.shape
    total[...] = jnp.zeros_like(total)
    for near in range(features_ref.shape[0]):
        for far in range(features_ref.shape[1]):
            j = block_of(near, far, blocks)
            product = matmul(tiles_ref[j].reshape(slots * side, side), features_ref[near, far])
            for slot in range(slots):
                row = rows_ref[slot, j]
                term = product[slot * side : (slot + 1) * side]
                total[lax.rem(row + rep, 2), row // 2] += jnp.where(slot < counts_ref[j], term, 0.0)
    kept_ref[...] = total[0]
    sent_ref[...] = total[1].astype(sent_ref.dtype)


def sum_parts(parts_ref, copies_ref):
    for place in range(2):
        total = parts_ref[place].astype(F32)
        for g in range(place + 2, parts_ref.shape[0], 2):
            total += parts_ref[g].astype(F32)
        copies_ref[place] = total.astype(BF16)
        copies_ref[place + 2] = total.astype(BF16)


def dense_layer(
    halves_ref, weight_ref, cotangent_ref, partner_ref, activations_ref, outgoing_ref
):
    side = cotangent_ref.shape[0]
    first = lax.rem(lax.axis_index("rep") // 2, 2) == 0
    aggregated = jnp.concatenate(
        [halves_ref[k].astype(F32) + halves_ref[k + 2].astype(F32) for k in range(2)], axis=0
    ).astype(BF16)
    cotangent, partner = cotangent_ref[...].astype(F32), partner_ref[...].astype(F32)
    cotangent = jnp.concatenate(
        [jnp.where(first, cotangent, partner), jnp.where(first, partner, cotangent)], axis=0
    )
    weight = weight_ref[...]
    pre = matmul(aggregated, weight)
    sigma = jax.nn.sigmoid(pre)
    activations = pre * sigma
    activations_ref[...] = jnp.where(first, activations[:side], activations[side:]).astype(BF16)
    grad_pre = (cotangent * sigma * (1.0 + pre * (1.0 - sigma))).astype(BF16)
    grad_agg = lax.dot_general(
        weight, grad_pre, (((1,), (1,)), ((), ())), preferred_element_type=F32
    ).astype(BF16)
    term = lax.dot_general(
        aggregated, grad_pre, (((0,), (0,)), ((), ())), preferred_element_type=F32
    )
    pieces = [
        term[top : top + 8, left : left + side]
        for top in range(0, term.shape[0], 8)
        for left in range(0, term.shape[1], side)
    ]
    count = len(pieces) // outgoing_ref.shape[0]
    for x in range(outgoing_ref.shape[0]):
        outgoing_ref[x, :side] = grad_agg[:, :side]
        outgoing_ref[x, side : 2 * side] = grad_agg[:, side:]
        lines = jnp.concatenate(pieces[x * count : (x + 1) * count], axis=0)
        outgoing_ref[x, 2 * side :] = lines.astype(BF16)


def backward_tiles(rows_ref, counts_ref, own_ref, other_ref, tiles_ref, outgoing_ref):
    rep = lax.axis_index("rep")
    blocks, slots, side, _ = tiles_ref.shape
    nears = outgoing_ref.shape[0]
    fars = blocks // nears
    grads = 2 * side
    own_sum, other_sum = own_ref[0, grads:].astype(F32), other_ref[0, grads:].astype(F32)
    for x in range(1, own_ref.shape[0]):
        own_sum += own_ref[x, grads:].astype(F32)
        other_sum += other_ref[x, grads:].astype(F32)
    carried = (own_sum + other_sum).astype(BF16)
    for near in range(nears):
        for far in range(fars):
            j = block_of(near, far, blocks)
            picked = []
            for slot in range(slots):
                row = rows_ref[slot, j]
                x = row // 4
                nodes = pl.ds(pl.multiple_of(lax.rem(row // 2, 2) * side, side), side)
                use_own = lax.rem(row + rep, 2) == 0
                block = jnp.where(use_own, own_ref[x, nodes], other_ref[x, nodes])
                picked.append(jnp.where(slot < counts_ref[j], block, jnp.zeros_like(block)))
            term = matmul(jnp.concatenate(picked, axis=1), tiles_ref[j].reshape(slots * side, side))
            outgoing_ref[near, far * side : (far + 1) * side] = term.astype(BF16)
        outgoing_ref[near, fars * side :] = carried


def relay_terms(arrived_ref, outgoing_ref):
    nears, _, side = arrived_ref.shape
    fars = outgoing_ref.shape[0]
    total = arrived_ref[0].astype(F32)
    for k in range(1, nears):
        total += arrived_ref[k].astype(F32)
    total = total.astype(BF16)
    for g in range(fars):
        outgoing_ref[g, :side] = total[g * side : (g + 1) * side]
        outgoing_ref[g, side:] = total[fars * side :]


def final_sums(parts_ref, feature_grad_ref, weight_ref):
    fars, _, side = parts_ref.shape
    total = parts_ref[0].astype(F32)
    for k in range(1, fars):
        total += parts_ref[k].astype(F32)
    feature_grad_ref[...] = total[:side].T.astype(BF16)
    for x in range(weight_ref.shape[0]):
        weight_ref[x] = total[side:]


def call(kernel, inputs, outputs, scratch=()):
    return pl.pallas_call(
        kernel,
        out_shape=outputs,
        in_specs=inputs,
        out_specs=[VMEM] * len(outputs),
        scratch_shapes=scratch,
        compiler_params=pltpu.CompilerParams(vmem_limit_bytes=32 * 2**20),
    )


def local(blocks, replicas, features, weight, cotangent, tile_vals, tile_row, tile_count):
    def shape(*dims, dtype=BF16):
        return jax.ShapeDtypeStruct(dims, dtype)

    side, width = features.shape
    hidden = weight.shape[1]
    nears, fars = 4, blocks // 4
    groups, x_size = replicas // 2, replicas // 4
    lines = weight.size // x_size // side
    tiles, rows, counts = tile_vals[0, 0], tile_row[0, 0].T, tile_count[0, 0]

    near_blocks = [[block_of(k, g, blocks) for k in range(nears)] for g in range(fars)]
    far_blocks = [[block_of(k, g, blocks) for g in range(fars)] for k in range(nears)]
    y_pairs = [[4 * x + c, 4 * x + 2 + c] for x in range(x_size) for c in range(2)]
    along_x = [[4 * x + k for x in range(x_size)] for k in range(4)]
    swap = [(r, r ^ 1) for r in range(replicas)]
    swap_y = [(r, r ^ 2) for r in range(replicas)]

    def exchange(block, axis, index_groups):
        return lax.all_to_all(block, axis, 0, 0, axis_index_groups=index_groups, tiled=True)

    with jax.named_scope("partner_cotangent"):
        partner = lax.ppermute(cotangent, "rep", swap_y)
    with jax.named_scope("gather_features"):
        (copies,) = call(spread, [VMEM], [shape(fars, side, width)])(features)
        band = exchange(copies, "blk", far_blocks)
        band, partner = lax.optimization_barrier((band, partner))
        (copies,) = call(spread, [VMEM], [shape(nears, fars, side, width)])(band)
        gathered = exchange(copies, "blk", near_blocks)
    kept, sent = call(
        forward_tiles,
        [SMEM, SMEM, VMEM, VMEM],
        [shape(groups, side, width, dtype=F32), shape(groups, side, width)],
        [pltpu.VMEM((2, groups, side, width), F32)],
    )(rows, counts, gathered, tiles)
    with jax.named_scope("sum_partials"):
        pair = (kept + lax.ppermute(sent, "rep", swap).astype(F32)).astype(BF16)
        parts = exchange(pair, "rep", along_x)
        (copies,) = call(sum_parts, [VMEM], [shape(4, side, width)])(parts)
        halves = exchange(copies, "rep", y_pairs)
    activations, outgoing = call(
        dense_layer,
        [VMEM] * 4,
        [shape(side, hidden), shape(x_size, 2 * side + lines, width)],
    )(halves, weight, cotangent, partner)
    with jax.named_scope("gather_grads"):
        own = exchange(outgoing, "rep", along_x)
        other = lax.ppermute(own, "rep", swap)
    (terms,) = call(
        backward_tiles,
        [SMEM, SMEM, VMEM, VMEM, VMEM],
        [shape(nears, fars * side + lines, width)],
    )(rows, counts, own, other, tiles)
    with jax.named_scope("sum_terms"):
        arrived = exchange(terms, "blk", near_blocks)
        (terms,) = call(relay_terms, [VMEM], [shape(fars, side + lines, width)])(arrived)
        arrived = exchange(terms, "blk", far_blocks)
    feature_grad, piece = call(
        final_sums,
        [VMEM],
        [shape(side, width), shape(x_size, lines, width, dtype=F32)],
    )(arrived)
    with jax.named_scope("gather_weight_grad"):
        pieces = exchange(piece, "rep", along_x).reshape(-1, hidden // side, 8, side)
    weight_grad = pieces.transpose(0, 2, 1, 3).reshape(weight.shape)
    return activations, feature_grad, weight_grad


def solution(mesh):
    in_specs = (
        P(("blk", "rep"), None),
        P(),
        P(("blk", "rep"), None),
        P("blk", "rep", None, None, None, None),
        P("blk", "rep", None, None),
        P("blk", "rep", None),
    )
    out_specs = (P(("blk", "rep"), None), P(("blk", "rep"), None), P())
    step = functools.partial(local, mesh.shape["blk"], mesh.shape["rep"])
    return jax.shard_map(step, mesh=mesh, in_specs=in_specs, out_specs=out_specs, check_vma=False)
```

```python
import functools

import jax
import jax.numpy as jnp
from jax import lax
from jax.experimental import pallas as pl
from jax.experimental.pallas import tpu as pltpu
from jax.sharding import PartitionSpec as P

VMEM = pl.BlockSpec(memory_space=pltpu.VMEM)
SMEM = pl.BlockSpec(memory_space=pltpu.SMEM)
F32 = jnp.float32
BF16 = jnp.bfloat16


def block_of(near, far, blocks):
    y_near, z_near = divmod(near, 2)
    y_far, z_far = divmod(far, blocks // 8)
    return ((y_far * 2 + y_near) * (blocks // 8) + z_far) * 2 + z_near


def matmul(a, b):
    return jnp.dot(a, b, preferred_element_type=F32)


def spread(block_ref, copies_ref):
    for k in range(copies_ref.shape[0]):
        copies_ref[k] = block_ref[...]


def forward_tiles(rows_ref, counts_ref, features_ref, tiles_ref, kept_ref, sent_ref, total):
    rep = lax.axis_index("rep")
    blocks, slots, side, _ = tiles_ref.shape
    total[...] = jnp.zeros_like(total)
    for near in range(features_ref.shape[0]):
        for far in range(features_ref.shape[1]):
            j = block_of(near, far, blocks)
            product = matmul(tiles_ref[j].reshape(slots * side, side), features_ref[near, far])
            for slot in range(slots):
                row = rows_ref[slot, j]
                term = product[slot * side : (slot + 1) * side]
                total[lax.rem(row + rep, 2), row // 2] += jnp.where(slot < counts_ref[j], term, 0.0)
    kept_ref[...] = total[0]
    sent_ref[...] = total[1].astype(sent_ref.dtype)


def sum_parts(parts_ref, cotangent_ref, sums_ref):
    side = parts_ref.shape[1]
    for place in range(2):
        total = parts_ref[place].astype(F32)
        for g in range(place + 2, parts_ref.shape[0], 2):
            total += parts_ref[g].astype(F32)
        sums_ref[place] = total.astype(BF16)
        sums_ref[2 + place] = cotangent_ref[:, place * side : (place + 1) * side]


def dense_layer(mine_ref, partner_ref, weight_ref, activations_ref, outgoing_ref):
    side = mine_ref.shape[1]
    first = lax.rem(lax.axis_index("rep") // 2, 2) == 0
    aggregated = jnp.concatenate(
        [mine_ref[k].astype(F32) + partner_ref[k].astype(F32) for k in range(2)], axis=0
    ).astype(BF16)
    mine = jnp.concatenate([mine_ref[2], mine_ref[3]], axis=1).astype(F32)
    partner = jnp.concatenate([partner_ref[2], partner_ref[3]], axis=1).astype(F32)
    cotangent = jnp.concatenate(
        [jnp.where(first, mine, partner), jnp.where(first, partner, mine)], axis=0
    )
    weight = weight_ref[...]
    pre = matmul(aggregated, weight)
    sigma = jax.nn.sigmoid(pre)
    activations = pre * sigma
    activations_ref[...] = jnp.where(first, activations[:side], activations[side:]).astype(BF16)
    grad_pre = (cotangent * sigma * (1.0 + pre * (1.0 - sigma))).astype(BF16)
    grad_agg = lax.dot_general(
        weight, grad_pre, (((1,), (1,)), ((), ())), preferred_element_type=F32
    ).astype(BF16)
    term = lax.dot_general(
        aggregated, grad_pre, (((0,), (0,)), ((), ())), preferred_element_type=F32
    )
    pieces = [
        term[top : top + 8, left : left + side]
        for top in range(0, term.shape[0], 8)
        for left in range(0, term.shape[1], side)
    ]
    count = len(pieces) // outgoing_ref.shape[0]
    for x in range(outgoing_ref.shape[0]):
        outgoing_ref[x, :side] = grad_agg[:, :side]
        outgoing_ref[x, side : 2 * side] = grad_agg[:, side:]
        lines = jnp.concatenate(pieces[x * count : (x + 1) * count], axis=0)
        outgoing_ref[x, 2 * side :] = lines.astype(BF16)


def backward_tiles(rows_ref, counts_ref, own_ref, other_ref, tiles_ref, outgoing_ref):
    rep = lax.axis_index("rep")
    blocks, slots, side, _ = tiles_ref.shape
    nears = outgoing_ref.shape[0]
    fars = blocks // nears
    grads = 2 * side
    own_sum, other_sum = own_ref[0, grads:].astype(F32), other_ref[0, grads:].astype(F32)
    for x in range(1, own_ref.shape[0]):
        own_sum += own_ref[x, grads:].astype(F32)
        other_sum += other_ref[x, grads:].astype(F32)
    carried = (own_sum + other_sum).astype(BF16)
    for near in range(nears):
        for far in range(fars):
            j = block_of(near, far, blocks)
            picked = []
            for slot in range(slots):
                row = rows_ref[slot, j]
                x = row // 4
                nodes = pl.ds(pl.multiple_of(lax.rem(row // 2, 2) * side, side), side)
                use_own = lax.rem(row + rep, 2) == 0
                block = jnp.where(use_own, own_ref[x, nodes], other_ref[x, nodes])
                picked.append(jnp.where(slot < counts_ref[j], block, jnp.zeros_like(block)))
            term = matmul(jnp.concatenate(picked, axis=1), tiles_ref[j].reshape(slots * side, side))
            outgoing_ref[near, far * side : (far + 1) * side] = term.astype(BF16)
        outgoing_ref[near, fars * side :] = carried


def relay_terms(arrived_ref, outgoing_ref):
    nears, _, side = arrived_ref.shape
    fars = outgoing_ref.shape[0]
    total = arrived_ref[0].astype(F32)
    for k in range(1, nears):
        total += arrived_ref[k].astype(F32)
    total = total.astype(BF16)
    for g in range(fars):
        outgoing_ref[g, :side] = total[g * side : (g + 1) * side]
        outgoing_ref[g, side:] = total[fars * side :]


def final_sums(parts_ref, feature_grad_ref, weight_ref):
    fars, _, side = parts_ref.shape
    total = parts_ref[0].astype(F32)
    for k in range(1, fars):
        total += parts_ref[k].astype(F32)
    feature_grad_ref[...] = total[:side].T.astype(BF16)
    for x in range(weight_ref.shape[0]):
        weight_ref[x] = total[side:]


def call(kernel, inputs, outputs, scratch=()):
    return pl.pallas_call(
        kernel,
        out_shape=outputs,
        in_specs=inputs,
        out_specs=[VMEM] * len(outputs),
        scratch_shapes=scratch,
        compiler_params=pltpu.CompilerParams(vmem_limit_bytes=32 * 2**20),
    )


def local(blocks, replicas, features, weight, cotangent, tile_vals, tile_row, tile_count):
    def shape(*dims, dtype=BF16):
        return jax.ShapeDtypeStruct(dims, dtype)

    side, width = features.shape
    hidden = weight.shape[1]
    nears, fars = 4, blocks // 4
    groups, x_size = replicas // 2, replicas // 4
    lines = weight.size // x_size // side
    tiles, rows, counts = tile_vals[0, 0], tile_row[0, 0].T, tile_count[0, 0]

    near_blocks = [[block_of(k, g, blocks) for k in range(nears)] for g in range(fars)]
    far_blocks = [[block_of(k, g, blocks) for g in range(fars)] for k in range(nears)]
    along_x = [[4 * x + k for x in range(x_size)] for k in range(4)]
    swap = [(r, r ^ 1) for r in range(replicas)]
    swap_y = [(r, r ^ 2) for r in range(replicas)]

    def exchange(block, axis, index_groups):
        return lax.all_to_all(block, axis, 0, 0, axis_index_groups=index_groups, tiled=True)

    with jax.named_scope("gather_features"):
        (copies,) = call(spread, [VMEM], [shape(fars, side, width)])(features)
        band = exchange(copies, "blk", far_blocks)
        (copies,) = call(spread, [VMEM], [shape(nears, fars, side, width)])(band)
        gathered = exchange(copies, "blk", near_blocks)
    kept, sent = call(
        forward_tiles,
        [SMEM, SMEM, VMEM, VMEM],
        [shape(groups, side, width, dtype=F32), shape(groups, side, width)],
        [pltpu.VMEM((2, groups, side, width), F32)],
    )(rows, counts, gathered, tiles)
    with jax.named_scope("sum_partials"):
        pair = (kept + lax.ppermute(sent, "rep", swap).astype(F32)).astype(BF16)
        parts = exchange(pair, "rep", along_x)
        (mine,) = call(sum_parts, [VMEM] * 2, [shape(4, side, width)])(parts, cotangent)
        partner = lax.ppermute(mine, "rep", swap_y)
    activations, outgoing = call(
        dense_layer,
        [VMEM] * 3,
        [shape(side, hidden), shape(x_size, 2 * side + lines, width)],
    )(mine, partner, weight)
    with jax.named_scope("gather_grads"):
        own = exchange(outgoing, "rep", along_x)
        other = lax.ppermute(own, "rep", swap)
    (terms,) = call(
        backward_tiles,
        [SMEM, SMEM, VMEM, VMEM, VMEM],
        [shape(nears, fars * side + lines, width)],
    )(rows, counts, own, other, tiles)
    with jax.named_scope("sum_terms"):
        arrived = exchange(terms, "blk", near_blocks)
        (terms,) = call(relay_terms, [VMEM], [shape(fars, side + lines, width)])(arrived)
        arrived = exchange(terms, "blk", far_blocks)
    feature_grad, piece = call(
        final_sums,
        [VMEM],
        [shape(side, width), shape(x_size, lines, width, dtype=F32)],
    )(arrived)
    with jax.named_scope("gather_weight_grad"):
        pieces = exchange(piece, "rep", along_x).reshape(-1, hidden // side, 8, side)
    weight_grad = pieces.transpose(0, 2, 1, 3).reshape(weight.shape)
    return activations, feature_grad, weight_grad


def solution(mesh):
    in_specs = (
        P(("blk", "rep"), None),
        P(),
        P(("blk", "rep"), None),
        P("blk", "rep", None, None, None, None),
        P("blk", "rep", None, None),
        P("blk", "rep", None),
    )
    out_specs = (P(("blk", "rep"), None), P(("blk", "rep"), None), P())
    step = functools.partial(local, mesh.shape["blk"], mesh.shape["rep"])
    return jax.shard_map(step, mesh=mesh, in_specs=in_specs, out_specs=out_specs, check_vma=False)
```
